512 devices in a mesh: dx: 16 (over z_lo, core), dy: 8 (over z_hi, x), tp: 4 (over y).
Axes of the slice: x: 4, y: 4, z: 16 (z_hi: 2, z_lo: 8; z = z_hi * 8 + z_lo), core: 2. Of those that a mesh axis runs over, the one named last changes fastest.
Arguments:
- normed: bfloat16 [16384, 4096], P(('dx', 'dy'), 'tp'), may hold values from -6 to 6
- key_weight: bfloat16 [4096, 512], P(None, 'tp'), may hold values from -0.09375 to 0.09375
- key_grad: bfloat16 [16384, 512], P(('dx', 'dy'), 'tp'), may hold values from -6 to 6
Outputs:
- input_grad: bfloat16 [16384, 4096], P(('dx', 'dy'), 'tp')
- weight_grad: bfloat16 [4096, 512], P(None, 'tp')
- bias_grad: float32 [512], P('tp')
The draws below stay inside these ranges and needn't reach their ends.
All inputs are finite; a program needn't handle non-finite values.
Results may differ from the reference program's by a relative error of at most 0.015.
Values may be sent and summed in bfloat16 or wider, within the bound.
A program may use at most 64 MiB of HBM per device.

```python
import math
import jax
import jax.numpy as jnp

D = 4096
HD = 128
SEQ = 4096
HEADS = 4
TOKENS = 16384
N_DX = 16
N_DY = 8


def levels(own_key, shape, split, least, top_value):
    level, own = 1.0, jax.random.fold_in(own_key, 6)
    for axis_at, shards_of in split:
        steps = jnp.exp(jax.random.uniform(jax.random.fold_in(own, axis_at), (shards_of,), jnp.float32, least / len(split), top_value / len(split)))
        level = level * jnp.repeat(steps, shape[axis_at] // shards_of).reshape([-1 if axis == axis_at else 1 for axis in range(len(shape))])
    return level


def scatter_about(key, extent, spread, bound, split=(), held_as=jnp.bfloat16):
    factor_of = levels(key, extent, split, -0.22, 0.18) if split else 1.0
    array = jax.random.normal(key, extent, jnp.float32) * spread * factor_of
    return jnp.minimum(jnp.maximum(array, -bound), bound).astype(held_as)


def setup_inputs(seed: int = 0) -> dict:
    splits = jax.random.split(jax.random.key(seed), 4)
    normed = scatter_about(splits[0], (TOKENS, D), 1.0, 6.0, ((0, 128), (1, 4)))
    key_weight = scatter_about(splits[1], (D, HEADS * HD), D ** -0.5, 0.09375, ((1, 4),))
    key_grad = scatter_about(splits[2], (TOKENS, HEADS * HD), 1.0, 6.0, ((0, 128), (1, 4)))
    return {"normed": normed, "key_weight": key_weight, "key_grad": key_grad}


def rope_back(grad, first_row):
    row_count = grad.shape[0]
    values = grad.astype(jnp.float32).reshape(row_count, -1, HD)
    half_size = HD // 2
    positions = ((first_row + jnp.arange(row_count, dtype=jnp.int32)) % SEQ).astype(jnp.float32)
    inverse_rates = jnp.exp(jnp.arange(half_size, dtype=jnp.float32) * (-2.0 * math.log(1000000.0) / HD))
    angles = positions[:, None] * inverse_rates[None, :]
    cosine = jnp.cos(angles)[:, None, :]
    sines = jnp.sin(angles)[:, None, :]
    first_half = values[:, :, :half_size]
    second_half = values[:, :, half_size:]
    result = jnp.concatenate([first_half * cosine + second_half * sines, second_half * cosine - first_half * sines], axis=2)
    return result.reshape(row_count, -1)


def reference(normed, key_weight, key_grad):
    replicas = N_DX * N_DY
    raw_grad = rope_back(key_grad, 0).astype(jnp.bfloat16)
    bias_grad = jnp.sum(raw_grad.astype(jnp.float32), axis=0) / replicas
    weight_sum = jnp.dot(normed.T, raw_grad, preferred_element_type=jnp.float32)
    weight_grad = (weight_sum / replicas).astype(jnp.bfloat16)
    total = jnp.zeros((raw_grad.shape[0], key_weight.shape[0]), jnp.float32)
    for head in range(HEADS):
        lo = head * HD
        part = jnp.dot(raw_grad[:, lo:lo + HD], key_weight[:, lo:lo + HD].T, preferred_element_type=jnp.float32)
        total = total + part.astype(jnp.bfloat16).astype(jnp.float32)
    input_grad = total.astype(jnp.bfloat16)
    return input_grad, weight_grad, bias_grad
```

```python
import math

import jax
import jax.numpy as jnp
from jax import lax
from jax.experimental import pallas as pl
from jax.experimental.pallas import tpu as pltpu
from jax.sharding import PartitionSpec as P

HD = 128
SEQ = 4096
HEADS = 4
ROWS = 128
WIDE = 1024
HALF = 512
MESH = pl.DeviceIdType.MESH
NEAR = [(kx, kz) for kz in range(2) for kx in range(4) if (kx, kz) != (0, 0)]
NEAR.sort(key=lambda k: -(min(k[0], 4 - k[0]) + k[1]))
ACROSS = [(ky, kc) for ky in (2, 1, 3, 0) for kc in (1, 0) if (ky, kc) != (0, 0)]
FAR = [4, 3, 5, 2, 6, 1, 7]


def rope_back(grad, first_row):
    values = grad.astype(jnp.float32)
    row = lax.broadcasted_iota(jnp.int32, (ROWS, HD), 0)
    lane = lax.broadcasted_iota(jnp.int32, (ROWS, HD), 1)
    positions = ((first_row + row) % SEQ).astype(jnp.float32)
    place = jnp.where(lane < HD // 2, lane, lane - HD // 2).astype(jnp.float32)
    angles = positions * jnp.exp(place * (-2.0 * math.log(1000000.0) / HD))
    sines = jnp.sin(angles)
    sines = jnp.where(lane < HD // 2, sines, -sines)
    return values * jnp.cos(angles) + pltpu.roll(values, HD // 2, 1) * sines


def kernel(
    normed, key_weight, key_grad, input_grad, weight_grad, bias_grad,
    keys, tokens, raw, weights, parts, got, halves, got_far, tile, inputs, bias_near, bias_far,
    load_sem, raw_send, raw_recv, normed_send, normed_recv, weight_send, weight_recv,
    near_send, near_recv, far_send, far_recv, tile_send, tile_recv, wide_send, wide_recv,
    core_send, core_recv, input_send, input_recv, input_own,
    bias_send, bias_recv, bias_far_send, bias_far_recv,
):
    dx, dy, y = lax.axis_index("dx"), lax.axis_index("dy"), lax.axis_index("tp")
    x, c = dy % 4, dx % 2
    z = (dy // 4) * 8 + dx // 2
    zp, zq = z % 2, z // 2
    xz = x * 2 + zp
    group, pair = zq // 2, zq % 2
    other = 1 - c

    def at(x, y, zq, zp, c):
        z = zq * 2 + zp
        return ((z % 8) * 2 + c, (z // 8) * 4 + x, y)

    def remote(source, target, send, recv, device):
        return pltpu.make_async_remote_copy(
            src_ref=source, dst_ref=target, send_sem=send, recv_sem=recv, device_id=device, device_id_type=MESH
        )

    sibling = at(x, y, zq, zp, other)
    barrier = pltpu.get_barrier_semaphore()
    partners = [at(x, y, (zq + k) % 8, zp, c) for k in FAR]
    partners += [at((x + kx) % 4, y, zq, (zp + kz) % 2, c) for kx, kz in NEAR]
    partners += [at(x, (y + ky) % 4, zq, zp, (c + kc) % 2) for ky, kc in ACROSS]
    for partner in partners:
        pl.semaphore_signal(barrier, inc=1, device_id=partner, device_id_type=MESH)

    own_half = pl.ds(pl.multiple_of(c * HALF, HALF), HALF)
    other_half = pl.ds(pl.multiple_of(other * HALF, HALF), HALF)
    own_head = pl.ds(pl.multiple_of(y * HD, HD), HD)
    load_keys = pltpu.make_async_copy(key_grad, keys, load_sem.at[0])
    load_normed = pltpu.make_async_copy(normed.at[:, own_half], tokens.at[c], load_sem.at[1])
    own_rows = pl.ds(pl.multiple_of(y * WIDE + c * HALF, HALF), HALF)
    load_weight = pltpu.make_async_copy(key_weight.at[own_rows], weights.at[:, own_head], load_sem.at[2])
    load_keys.start()
    load_normed.start()
    load_weight.start()
    load_keys.wait()
    first_row = (dx * 8 + dy) * ROWS
    raw[c, :, own_head] = rope_back(keys[...], first_row).astype(jnp.bfloat16)

    pl.semaphore_wait(barrier, len(partners))

    raw_copies = [
        remote(raw.at[c, :, own_head], raw.at[c, :, own_head], raw_send.at[i], raw_recv.at[i],
               at(x, (y + ky) % 4, zq, zp, (c + kc) % 2))
        for i, (ky, kc) in enumerate(ACROSS)
    ]
    for copy in raw_copies:
        copy.start()
    normed_copy = remote(normed.at[:, other_half], tokens.at[c], normed_send, normed_recv, sibling)
    normed_copy.start()
    weight_copies = []
    for i, ky in enumerate((2, 1, 3)):
        there = (y + ky) % 4
        rows = pl.ds(pl.multiple_of(there * WIDE + c * HALF, HALF), HALF)
        weight_copies.append(
            remote(key_weight.at[rows], weights.at[:, own_head], weight_send.at[i], weight_recv.at[i],
                   at(x, there, zq, zp, c))
        )
    for copy in weight_copies:
        copy.start()
    load_normed.wait()
    normed_copy.wait_recv()
    for copy in raw_copies:
        copy.wait_recv()

    product = lax.dot_general(
        tokens[...].reshape(2 * ROWS, HALF), raw[...].reshape(2 * ROWS, HEADS * HD),
        (((0,), (0,)), ((), ())), preferred_element_type=jnp.float32,
    )
    parts[...] = product.astype(jnp.bfloat16).reshape(8, 64, HEADS * HD)
    near_copies = []
    for i, (kx, kz) in enumerate(NEAR):
        there = ((x + kx) % 4) * 2 + (zp + kz) % 2
        near_copies.append(
            remote(parts.at[there], got.at[xz], near_send.at[i], near_recv.at[i],
                   at((x + kx) % 4, y, zq, (zp + kz) % 2, c))
        )
    for copy in near_copies:
        copy.start()
    got[xz] = parts[xz]

    raw_head = raw[:, :, own_head].astype(jnp.float32).reshape(2 * ROWS, HD)
    bias_near[xz] = jnp.broadcast_to(jnp.sum(raw_head, axis=0, keepdims=True), (8, HD))
    bias_copies = [
        remote(bias_near.at[xz], bias_near.at[xz], bias_send.at[i], bias_recv.at[i],
               at((x + kx) % 4, y, zq, (zp + kz) % 2, c))
        for i, (kx, kz) in enumerate(NEAR)
    ]
    for copy in bias_copies:
        copy.start()

    for copy in near_copies:
        copy.wait_recv()
    total = got[0].astype(jnp.float32)
    for s in range(1, 8):
        total += got[s].astype(jnp.float32)
    total = total.astype(jnp.bfloat16)
    for s in range(8):
        halves[s] = total[(s // 2) * 16:(s // 2) * 16 + 16, (s % 2) * 256:(s % 2) * 256 + 256]
    far_copies = [
        remote(halves.at[(zq + k) % 8], got_far.at[zq], far_send.at[i], far_recv.at[i], at(x, y, (zq + k) % 8, zp, c))
        for i, k in enumerate(FAR)
    ]
    for copy in far_copies:
        copy.start()
    got_far[zq] = halves[zq]

    for copy in bias_copies:
        copy.wait()
    bias_part = bias_near[0]
    for s in range(1, 8):
        bias_part += bias_near[s]
    bias_far[zq] = bias_part
    bias_far_copies = [
        remote(bias_far.at[zq], bias_far.at[zq], bias_far_send.at[i], bias_far_recv.at[i],
               at(x, y, (zq + k) % 8, zp, c))
        for i, k in enumerate(FAR)
    ]
    for copy in bias_far_copies:
        copy.start()

    load_weight.wait()
    for copy in weight_copies:
        copy.wait()
    result = lax.dot_general(
        raw[...].reshape(2 * ROWS, HEADS * HD), weights[...],
        (((1,), (1,)), ((), ())), preferred_element_type=jnp.float32,
    )
    inputs[...] = result.astype(jnp.bfloat16).reshape(2, ROWS, HALF)
    input_copy = remote(inputs.at[other], input_grad.at[:, own_half], input_send, input_recv, sibling)
    input_copy.start()
    input_local = pltpu.make_async_copy(inputs.at[c], input_grad.at[:, own_half], input_own)
    input_local.start()

    for copy in far_copies:
        copy.wait_recv()
    final = got_far[0].astype(jnp.float32)
    for s in range(1, 8):
        final += got_far[s].astype(jnp.float32)
    final = (final * (1.0 / 128.0)).astype(jnp.bfloat16)
    tile[0] = final[:, :HD]
    tile[1] = final[:, HD:]

    target = weight_grad.at[y, c, xz, group]
    tile_copies = []
    for k in FAR + [0]:
        for h in range(2):
            i = len(tile_copies)
            there = pair * 2 + h
            tile_copies.append(
                (remote(tile.at[h], target, tile_send.at[i], tile_recv, at(x, there, (zq + k) % 8, zp, c)), k, there)
            )
    own_tiles = [pltpu.make_async_copy(tile.at[h], target, tile_recv) for h in range(2)]
    for copy, k, there in tile_copies:
        if k:
            copy.start()
        else:
            pl.when(there != y)(copy.start)
    for h in range(2):
        pl.when(pair * 2 + h == y)(own_tiles[h].start)

    for copy in bias_far_copies:
        copy.wait()
    bias_all = bias_far[0]
    for s in range(1, 8):
        bias_all += bias_far[s]
    bias_grad[...] = bias_all[0:1] * (1.0 / 128.0)

    own_block = weight_grad.at[:, c, xz]
    pltpu.make_async_copy(own_block, own_block, tile_recv).wait()

    wide_copies = [
        remote(own_block, own_block, wide_send.at[i], wide_recv.at[i], at((x + kx) % 4, y, zq, (zp + kz) % 2, c))
        for i, (kx, kz) in enumerate(NEAR)
    ]
    for copy in wide_copies:
        copy.start()
    core_copies = [remote(own_block, own_block, core_send.at[7], core_recv.at[7], sibling)]
    core_copies[0].start()
    order = sorted(range(7), key=lambda i: -i)
    for i in order:
        kx, kz = NEAR[i]
        came = weight_grad.at[:, c, ((x - kx) % 4) * 2 + (zp - kz) % 2]
        wide_copies[i].wait_recv()
        forward = remote(came, came, core_send.at[i], core_recv.at[i], sibling)
        forward.start()
        core_copies.append(forward)
    for copy in core_copies:
        copy.wait()
    for copy in wide_copies + near_copies + far_copies + raw_copies + [normed_copy]:
        copy.wait_send()
    for copy, k, there in tile_copies:
        if k:
            copy.wait_send()
        else:
            pl.when(there != y)(copy.wait_send)
    input_copy.wait()
    input_local.wait()


def body(normed, key_weight, key_grad):
    dma = pltpu.SemaphoreType.DMA
    bf16, f32 = jnp.bfloat16, jnp.float32
    anywhere = pl.BlockSpec(memory_space=pl.ANY)
    input_grad, weight_grad, bias_grad = pl.pallas_call(
        kernel,
        out_shape=(
            jax.ShapeDtypeStruct((ROWS, WIDE), bf16),
            jax.ShapeDtypeStruct((4, 2, 8, 4, 16, HD), bf16),
            jax.ShapeDtypeStruct((1, HD), f32),
        ),
        in_specs=[anywhere] * 3,
        out_specs=(anywhere, anywhere, pl.BlockSpec(memory_space=pltpu.VMEM)),
        scratch_shapes=[
            pltpu.VMEM((ROWS, HD), bf16),
            pltpu.VMEM((2, ROWS, HALF), bf16),
            pltpu.VMEM((2, ROWS, HEADS * HD), bf16),
            pltpu.VMEM((HALF, HEADS * HD), bf16),
            pltpu.VMEM((8, 64, HEADS * HD), bf16),
            pltpu.VMEM((8, 64, HEADS * HD), bf16),
            pltpu.VMEM((8, 16, 2 * HD), bf16),
            pltpu.VMEM((8, 16, 2 * HD), bf16),
            pltpu.VMEM((2, 16, HD), bf16),
            pltpu.VMEM((2, ROWS, HALF), bf16),
            pltpu.VMEM((8, 8, HD), f32),
            pltpu.VMEM((8, 8, HD), f32),
            dma((3,)), dma((7,)), dma((7,)), dma, dma, dma((3,)), dma((3,)),
            dma((7,)), dma((7,)), dma((7,)), dma((7,)), dma((16,)), dma, dma((7,)), dma((7,)),
            dma((8,)), dma((8,)), dma, dma, dma,
            dma((7,)), dma((7,)), dma((7,)), dma((7,)),
        ],
        compiler_params=pltpu.CompilerParams(collective_id=0, has_side_effects=True, vmem_limit_bytes=32 << 20),
        cost_estimate=pl.CostEstimate(flops=4 * 256 * 512 * 512, bytes_accessed=4 << 20, transcendentals=0),
        name="key_projection_backward",
    )(normed, key_weight, key_grad)
    return input_grad, weight_grad.reshape(4096, HD), bias_grad.reshape(HD)


def solution(mesh):
    placed = (P(("dx", "dy"), "tp"), P(None, "tp"), P(("dx", "dy"), "tp"))
    return jax.shard_map(
        body,
        mesh=mesh,
        in_specs=placed,
        out_specs=(P(("dx", "dy"), "tp"), P(None, "tp"), P("tp")),
        check_vma=False,
    )
```

```python
import math

import jax
import jax.numpy as jnp
from jax import lax
from jax.experimental import pallas as pl
from jax.experimental.pallas import tpu as pltpu
from jax.sharding import PartitionSpec as P

HD = 128
SEQ = 4096
HEADS = 4
ROWS = 128
WIDE = 1024
HALF = 512
MESH = pl.DeviceIdType.MESH
NEAR = [(kx, kz) for kz in range(2) for kx in range(4) if (kx, kz) != (0, 0)]
NEAR.sort(key=lambda k: -(min(k[0], 4 - k[0]) + k[1]))
ACROSS = [(ky, kc) for ky in (2, 1, 3, 0) for kc in (1, 0) if (ky, kc) != (0, 0)]
FAR = [4, 3, 5, 2, 6, 1, 7]
GROUPS = 4


def rope_back(grad, first_row):
    values = grad.astype(jnp.float32)
    row = lax.broadcasted_iota(jnp.int32, (ROWS, HD), 0)
    lane = lax.broadcasted_iota(jnp.int32, (ROWS, HD), 1)
    positions = ((first_row + row) % SEQ).astype(jnp.float32)
    place = jnp.where(lane < HD // 2, lane, lane - HD // 2).astype(jnp.float32)
    angles = positions * jnp.exp(place * (-2.0 * math.log(1000000.0) / HD))
    sines = jnp.sin(angles)
    sines = jnp.where(lane < HD // 2, sines, -sines)
    return values * jnp.cos(angles) + pltpu.roll(values, HD // 2, 1) * sines


def kernel(
    normed, key_weight, key_grad, input_grad, weight_grad, bias_grad,
    keys, tokens, turned, raw, weights, parts, got, halves, got_far, tile, inputs, bias_near, bias_far,
    load_sem, raw_send, raw_recv, normed_send, normed_recv, weight_send, weight_recv,
    near_send, near_recv, far_send, far_recv, tile_send, tile_recv, wide_send, wide_recv,
    core_send, core_recv, input_send, input_recv, input_own,
    bias_send, bias_recv, bias_far_send, bias_far_recv, one_away, two_away,
):
    dx, dy, y = lax.axis_index("dx"), lax.axis_index("dy"), lax.axis_index("tp")
    x, c = dy % 4, dx % 2
    z = (dy // 4) * 8 + dx // 2
    zp, zq = z % 2, z // 2
    xz = x * 2 + zp
    group, pair = zq // 2, zq % 2
    other = 1 - c

    def at(x, y, zq, zp, c):
        z = zq * 2 + zp
        return ((z % 8) * 2 + c, (z // 8) * 4 + x, y)

    def along(k):
        return at(x, y, (zq + k) % 8, zp, c)

    def near(kx, kz):
        return at((x + kx) % 4, y, zq, (zp + kz) % 2, c)

    def signal(semaphore, device):
        pl.semaphore_signal(semaphore, inc=1, device_id=device, device_id_type=MESH)

    def remote(source, target, send, recv, device):
        return pltpu.make_async_remote_copy(
            src_ref=source, dst_ref=target, send_sem=send, recv_sem=recv, device_id=device, device_id_type=MESH
        )

    sibling = at(x, y, zq, zp, other)
    barrier = pltpu.get_barrier_semaphore()
    partners = [along(1), along(7)] + [near(kx, kz) for kx, kz in NEAR]
    partners += [at(x, (y + ky) % 4, zq, zp, (c + kc) % 2) for ky, kc in ACROSS]
    for partner in partners:
        signal(barrier, partner)

    own_half = pl.ds(pl.multiple_of(c * HALF, HALF), HALF)
    other_half = pl.ds(pl.multiple_of(other * HALF, HALF), HALF)
    own_head = pl.ds(pl.multiple_of(y * HD, HD), HD)
    load_keys = pltpu.make_async_copy(key_grad, keys, load_sem.at[0])
    load_normed = pltpu.make_async_copy(normed.at[:, own_half], tokens.at[c], load_sem.at[1])
    own_rows = pl.ds(pl.multiple_of(y * WIDE + c * HALF, HALF), HALF)
    load_weight = pltpu.make_async_copy(key_weight.at[own_rows], weights.at[:, own_head], load_sem.at[2])
    load_keys.start()
    load_normed.start()
    load_weight.start()
    load_keys.wait()
    first_row = (dx * 8 + dy) * ROWS
    raw[c, :, own_head] = rope_back(keys[...], first_row).astype(jnp.bfloat16)

    pl.semaphore_wait(barrier, len(partners))

    raw_copies = [
        remote(raw.at[c, :, own_head], raw.at[c, :, own_head], raw_send.at[i], raw_recv.at[i],
               at(x, (y + ky) % 4, zq, zp, (c + kc) % 2))
        for i, (ky, kc) in enumerate(ACROSS)
    ]
    for copy in raw_copies:
        copy.start()
    normed_copy = remote(normed.at[:, other_half], tokens.at[c], normed_send, normed_recv, sibling)
    normed_copy.start()
    for k in (1, 7):
        signal(one_away, along(k))
    load_normed.wait()
    normed_copy.wait_recv()
    turned[...] = tokens[...].reshape(2 * ROWS, HALF).T
    pl.semaphore_wait(one_away, 2)
    for k in (2, 6):
        signal(two_away, along(k))
    for copy in raw_copies:
        copy.wait_recv()

    product = jnp.dot(
        turned[...], raw[...].reshape(2 * ROWS, HEADS * HD), preferred_element_type=jnp.float32
    )
    parts[...] = product.astype(jnp.bfloat16).reshape(8, GROUPS, 16, HEADS * HD)
    step = 1 + 2 * pair
    order = [(group + 2) % 4, (group + step) % 4, (group + 4 - step) % 4, group]
    near_copies = [
        [
            remote(parts.at[((x + kx) % 4) * 2 + (zp + kz) % 2, g], got.at[xz, g],
                   near_send.at[j, i], near_recv.at[j, i], near(kx, kz))
            for i, (kx, kz) in enumerate(NEAR)
        ]
        for j, g in enumerate(order)
    ]
    for copies in near_copies:
        for copy in copies:
            copy.start()
    got[xz] = parts[xz]

    raw_head = raw[:, :, own_head].astype(jnp.float32).reshape(2 * ROWS, HD)
    bias_near[xz] = jnp.broadcast_to(jnp.sum(raw_head, axis=0, keepdims=True), (8, HD))
    bias_copies = [
        remote(bias_near.at[xz], bias_near.at[xz], bias_send.at[i], bias_recv.at[i], near(kx, kz))
        for i, (kx, kz) in enumerate(NEAR)
    ]
    for copy in bias_copies:
        copy.start()

    pl.semaphore_wait(two_away, 2)
    far_copies = []
    for j, g in enumerate(order):
        for copy in near_copies[j]:
            copy.wait_recv()
        total = got[0, g].astype(jnp.float32)
        for s in range(1, 8):
            total += got[s, g].astype(jnp.float32)
        total = total.astype(jnp.bfloat16)
        for h in range(2):
            halves[g * 2 + h] = total[:, h * 256:h * 256 + 256]
        for h in range(2 if j < 3 else 1):
            there = g * 2 + h if j < 3 else g * 2 + 1 - pair
            copy = remote(halves.at[there], got_far.at[zq], far_send.at[len(far_copies)], far_recv,
                          at(x, y, there, zp, c))
            copy.start()
            far_copies.append(copy)
    got_far[zq] = halves[zq]

    weight_copies = []
    for i, ky in enumerate((2, 1, 3)):
        there = (y + ky) % 4
        rows = pl.ds(pl.multiple_of(there * WIDE + c * HALF, HALF), HALF)
        weight_copies.append(
            remote(key_weight.at[rows], weights.at[:, own_head], weight_send.at[i], weight_recv.at[i],
                   at(x, there, zq, zp, c))
        )
    for copy in weight_copies:
        copy.start()

    for copy in bias_copies:
        copy.wait()
    bias_part = bias_near[0]
    for s in range(1, 8):
        bias_part += bias_near[s]
    bias_far[zq] = bias_part
    bias_far_copies = [
        remote(bias_far.at[zq], bias_far.at[zq], bias_far_send.at[i], bias_far_recv.at[i], along(k))
        for i, k in enumerate(FAR)
    ]
    for copy in bias_far_copies:
        copy.start()

    arrived = got_far.at[pl.ds(0, 7)]
    pltpu.make_async_copy(arrived, arrived, far_recv).wait()
    final = got_far[0].astype(jnp.float32)
    for s in range(1, 8):
        final += got_far[s].astype(jnp.float32)
    final = (final * (1.0 / 128.0)).astype(jnp.bfloat16)
    tile[0] = final[:, :HD]
    tile[1] = final[:, HD:]

    target = weight_grad.at[y, c, xz, group]
    tile_copies = []
    for k in FAR + [0]:
        for h in range(2):
            there = pair * 2 + h
            copy = remote(tile.at[h], target, tile_send.at[len(tile_copies)], tile_recv.at[group],
                          at(x, there, (zq + k) % 8, zp, c))
            tile_copies.append((copy, k, there))
    own_tiles = [pltpu.make_async_copy(tile.at[h], target, tile_recv.at[group]) for h in range(2)]
    for copy, k, there in tile_copies:
        if k:
            copy.start()
        else:
            pl.when(there != y)(copy.start)
    for h in range(2):
        pl.when(pair * 2 + h == y)(own_tiles[h].start)

    load_weight.wait()
    for copy in weight_copies:
        copy.wait_recv()
    result = lax.dot_general(
        raw[...].reshape(2 * ROWS, HEADS * HD), weights[...],
        (((1,), (1,)), ((), ())), preferred_element_type=jnp.float32,
    )
    inputs[...] = result.astype(jnp.bfloat16).reshape(2, ROWS, HALF)
    input_copy = remote(inputs.at[other], input_grad.at[:, own_half], input_send, input_recv, sibling)
    input_copy.start()
    input_local = pltpu.make_async_copy(inputs.at[c], input_grad.at[:, own_half], input_own)
    input_local.start()

    arrivals = [group, (group + 1) % 4, (group + 3) % 4, (group + 2) % 4]
    wide_copies = []
    for j, g in enumerate(arrivals):
        block = weight_grad.at[:, c, xz, g]
        pltpu.make_async_copy(block, block, tile_recv.at[g]).wait()
        copies = [
            remote(block, block, wide_send.at[j, i], wide_recv.at[j, i], near(kx, kz))
            for i, (kx, kz) in enumerate(NEAR)
        ]
        for copy in copies:
            copy.start()
        wide_copies.append(copies)

    for copy in bias_far_copies:
        copy.wait()
    bias_all = bias_far[0]
    for s in range(1, 8):
        bias_all += bias_far[s]
    bias_grad[...] = bias_all[0:1] * (1.0 / 128.0)

    core_copies = []
    for j, g in enumerate(arrivals):
        for copy in wide_copies[j]:
            copy.wait_recv()
        block = weight_grad.at[:, c, :, g]
        copy = remote(block, block, core_send.at[j], core_recv.at[j], sibling)
        copy.start()
        core_copies.append(copy)

    for copy in raw_copies + [normed_copy] + sum(near_copies, []) + far_copies + weight_copies + sum(wide_copies, []):
        copy.wait_send()
    for copy, k, there in tile_copies:
        if k:
            copy.wait_send()
        else:
            pl.when(there != y)(copy.wait_send)
    input_copy.wait()
    input_local.wait()
    for copy in core_copies:
        copy.wait()


def finish(input_vmem, weight_vmem, bias_vmem, input_grad, weight_grad, bias_grad, done):
    copies = [
        pltpu.make_async_copy(weight_vmem, weight_grad, done.at[0]),
        pltpu.make_async_copy(input_vmem, input_grad, done.at[1]),
        pltpu.make_async_copy(bias_vmem, bias_grad, done.at[2]),
    ]
    for copy in copies:
        copy.start()
    for copy in copies:
        copy.wait()


def body(normed, key_weight, key_grad):
    dma, regular = pltpu.SemaphoreType.DMA, pltpu.SemaphoreType.REGULAR
    bf16, f32 = jnp.bfloat16, jnp.float32
    hbm = pl.BlockSpec(memory_space=pltpu.HBM)
    anywhere = pl.BlockSpec(memory_space=pl.ANY)
    local = pl.BlockSpec(memory_space=pltpu.VMEM)
    shapes = (
        jax.ShapeDtypeStruct((ROWS, WIDE), bf16),
        jax.ShapeDtypeStruct((4, 2, 8, GROUPS, 16, HD), bf16),
        jax.ShapeDtypeStruct((1, HD), f32),
    )
    normed, key_weight, key_grad = (pltpu.with_memory_space_constraint(a, pltpu.HBM) for a in (normed, key_weight, key_grad))
    results = pl.pallas_call(
        kernel,
        out_shape=shapes,
        in_specs=[hbm] * 3,
        out_specs=(anywhere, anywhere, local),
        scratch_shapes=[
            pltpu.VMEM((ROWS, HD), bf16),
            pltpu.VMEM((2, ROWS, HALF), bf16),
            pltpu.VMEM((HALF, 2 * ROWS), bf16),
            pltpu.VMEM((2, ROWS, HEADS * HD), bf16),
            pltpu.VMEM((HALF, HEADS * HD), bf16),
            pltpu.VMEM((8, GROUPS, 16, HEADS * HD), bf16),
            pltpu.VMEM((8, GROUPS, 16, HEADS * HD), bf16),
            pltpu.VMEM((8, 16, 2 * HD), bf16),
            pltpu.VMEM((8, 16, 2 * HD), bf16),
            pltpu.VMEM((2, 16, HD), bf16),
            pltpu.VMEM((2, ROWS, HALF), bf16),
            pltpu.VMEM((8, 8, HD), f32),
            pltpu.VMEM((8, 8, HD), f32),
            dma((3,)), dma((7,)), dma((7,)), dma, dma, dma((3,)), dma((3,)),
            dma((4, 7)), dma((4, 7)), dma((7,)), dma, dma((16,)), dma((4,)), dma((4, 7)), dma((4, 7)),
            dma((4,)), dma((4,)), dma, dma, dma,
            dma((7,)), dma((7,)), dma((7,)), dma((7,)), regular, regular,
        ],
        compiler_params=pltpu.CompilerParams(collective_id=0, has_side_effects=True, vmem_limit_bytes=32 << 20),
        cost_estimate=pl.CostEstimate(flops=4 * 256 * 512 * 512, bytes_accessed=4 << 20, transcendentals=0),
        name="key_projection_backward",
    )(normed, key_weight, key_grad)
    input_grad, weight_grad, bias_grad = pl.pallas_call(
        finish,
        out_shape=shapes,
        in_specs=[anywhere] * 3,
        out_specs=(hbm,) * 3,
        scratch_shapes=[dma((3,))],
        name="write_results",
    )(*results)
    return input_grad, weight_grad.reshape(4096, HD), bias_grad.reshape(HD)


def solution(mesh):
    placed = (P(("dx", "dy"), "tp"), P(None, "tp"), P(("dx", "dy"), "tp"))
    return jax.shard_map(
        body,
        mesh=mesh,
        in_specs=placed,
        out_specs=(P(("dx", "dy"), "tp"), P(None, "tp"), P("tp")),
        check_vma=False,
    )
```

```python
import math

import jax
import jax.numpy as jnp
from jax import lax
from jax.experimental import pallas as pl
from jax.experimental.pallas import tpu as pltpu
from jax.sharding import PartitionSpec as P

HD = 128
SEQ = 4096
HEADS = 4
ROWS = 128
WIDE = 1024
HALF = 512
MESH = pl.DeviceIdType.MESH
NEAR = [(kx, kz) for kz in range(2) for kx in range(4) if (kx, kz) != (0, 0)]
NEAR.sort(key=lambda k: -(min(k[0], 4 - k[0]) + k[1]))
ACROSS = [(ky, kc) for ky in (2, 1, 3, 0) for kc in (1, 0) if (ky, kc) != (0, 0)]
FAR = [4, 3, 5, 2, 6, 1, 7]
GROUPS = 4


def rope_back(grad, first_row):
    values = grad.astype(jnp.float32)
    row = lax.broadcasted_iota(jnp.int32, (ROWS, HD), 0)
    lane = lax.broadcasted_iota(jnp.int32, (ROWS, HD), 1)
    positions = ((first_row + row) % SEQ).astype(jnp.float32)
    place = jnp.where(lane < HD // 2, lane, lane - HD // 2).astype(jnp.float32)
    angles = positions * jnp.exp(place * (-2.0 * math.log(1000000.0) / HD))
    sines = jnp.sin(angles)
    sines = jnp.where(lane < HD // 2, sines, -sines)
    return values * jnp.cos(angles) + pltpu.roll(values, HD // 2, 1) * sines


def kernel(
    normed, key_weight, key_grad, input_grad, weight_grad, bias_grad,
    keys, tokens, turned, raw, weights, parts, got, halves, got_far, tile, inputs, bias_near, bias_far,
    load_sem, raw_send, raw_recv, normed_send, normed_recv, weight_send, weight_recv,
    near_send, near_recv, far_send, far_recv, tile_send, tile_recv, wide_send, wide_recv,
    core_send, core_recv, input_send, input_recv, input_own,
    bias_send, bias_recv, bias_far_send, bias_far_recv, one_away, two_away,
):
    dx, dy, y = lax.axis_index("dx"), lax.axis_index("dy"), lax.axis_index("tp")
    x, c = dy % 4, dx % 2
    z = (dy // 4) * 8 + dx // 2
    zp, zq = z % 2, z // 2
    xz = x * 2 + zp
    group, pair = zq // 2, zq % 2
    other = 1 - c

    def at(x, y, zq, zp, c):
        z = zq * 2 + zp
        return ((z % 8) * 2 + c, (z // 8) * 4 + x, y)

    def along(k):
        return at(x, y, (zq + k) % 8, zp, c)

    def near(kx, kz):
        return at((x + kx) % 4, y, zq, (zp + kz) % 2, c)

    def signal(semaphore, device):
        pl.semaphore_signal(semaphore, inc=1, device_id=device, device_id_type=MESH)

    def remote(source, target, send, recv, device):
        return pltpu.make_async_remote_copy(
            src_ref=source, dst_ref=target, send_sem=send, recv_sem=recv, device_id=device, device_id_type=MESH
        )

    sibling = at(x, y, zq, zp, other)
    barrier = pltpu.get_barrier_semaphore()
    partners = [along(1), along(7)] + [near(kx, kz) for kx, kz in NEAR]
    partners += [at(x, (y + ky) % 4, zq, zp, (c + kc) % 2) for ky, kc in ACROSS]
    for partner in partners:
        signal(barrier, partner)

    own_half = pl.ds(pl.multiple_of(c * HALF, HALF), HALF)
    other_half = pl.ds(pl.multiple_of(other * HALF, HALF), HALF)
    own_head = pl.ds(pl.multiple_of(y * HD, HD), HD)
    load_keys = pltpu.make_async_copy(key_grad, keys, load_sem.at[0])
    load_normed = pltpu.make_async_copy(normed.at[:, own_half], tokens.at[c], load_sem.at[1])
    own_rows = pl.ds(pl.multiple_of(y * WIDE + c * HALF, HALF), HALF)
    load_weight = pltpu.make_async_copy(key_weight.at[own_rows], weights.at[:, own_head], load_sem.at[2])
    load_keys.start()
    load_normed.start()
    load_weight.start()
    load_keys.wait()
    first_row = (dx * 8 + dy) * ROWS
    raw[c, :, own_head] = rope_back(keys[...], first_row).astype(jnp.bfloat16)

    pl.semaphore_wait(barrier, len(partners))

    raw_copies = [
        remote(raw.at[c, :, own_head], raw.at[c, :, own_head], raw_send.at[i], raw_recv.at[i],
               at(x, (y + ky) % 4, zq, zp, (c + kc) % 2))
        for i, (ky, kc) in enumerate(ACROSS)
    ]
    for copy in raw_copies:
        copy.start()
    normed_copy = remote(normed.at[:, other_half], tokens.at[c], normed_send, normed_recv, sibling)
    normed_copy.start()
    for k in (1, 7):
        signal(one_away, along(k))
    load_normed.wait()
    normed_copy.wait_recv()
    turned[...] = tokens[...].reshape(2 * ROWS, HALF).T
    pl.semaphore_wait(one_away, 2)
    for k in (2, 6):
        signal(two_away, along(k))
    for copy in raw_copies:
        copy.wait_recv()

    product = jnp.dot(
        turned[...], raw[...].reshape(2 * ROWS, HEADS * HD), preferred_element_type=jnp.float32
    )
    parts[...] = product.astype(jnp.bfloat16).reshape(8, GROUPS, 16, HEADS * HD)
    step = 1 + 2 * pair
    order = [(group + 2) % 4, (group + step) % 4, (group + 4 - step) % 4, group]
    near_copies = [
        [
            remote(parts.at[((x + kx) % 4) * 2 + (zp + kz) % 2, g], got.at[xz, g],
                   near_send.at[j, i], near_recv.at[j, i], near(kx, kz))
            for i, (kx, kz) in enumerate(NEAR)
        ]
        for j, g in enumerate(order)
    ]
    for copies in near_copies:
        for copy in copies:
            copy.start()
    got[xz] = parts[xz]

    raw_head = raw[:, :, own_head].astype(jnp.float32).reshape(2 * ROWS, HD)
    bias_near[xz] = jnp.broadcast_to(jnp.sum(raw_head, axis=0, keepdims=True), (8, HD))
    bias_copies = [
        remote(bias_near.at[xz], bias_near.at[xz], bias_send.at[i], bias_recv.at[i], near(kx, kz))
        for i, (kx, kz) in enumerate(NEAR)
    ]
    for copy in bias_copies:
        copy.start()

    pl.semaphore_wait(two_away, 2)
    far_copies = []
    for j, g in enumerate(order):
        for copy in near_copies[j]:
            copy.wait_recv()
        total = got[0, g].astype(jnp.float32)
        for s in range(1, 8):
            total += got[s, g].astype(jnp.float32)
        total = total.astype(jnp.bfloat16)
        for h in range(2):
            halves[g * 2 + h] = total[:, h * 256:h * 256 + 256]
        for h in range(2 if j < 3 else 1):
            there = g * 2 + h if j < 3 else g * 2 + 1 - pair
            copy = remote(halves.at[there], got_far.at[zq], far_send.at[len(far_copies)], far_recv,
                          at(x, y, there, zp, c))
            copy.start()
            far_copies.append(copy)
    got_far[zq] = halves[zq]

    weight_copies = []
    for i, ky in enumerate((2, 1, 3)):
        there = (y + ky) % 4
        rows = pl.ds(pl.multiple_of(there * WIDE + c * HALF, HALF), HALF)
        weight_copies.append(
            remote(key_weight.at[rows], weights.at[:, own_head], weight_send.at[i], weight_recv.at[i],
                   at(x, there, zq, zp, c))
        )
    for copy in weight_copies:
        copy.start()

    for copy in bias_copies:
        copy.wait()
    bias_part = bias_near[0]
    for s in range(1, 8):
        bias_part += bias_near[s]
    bias_far[zq] = bias_part
    bias_far_copies = [
        remote(bias_far.at[zq], bias_far.at[zq], bias_far_send.at[i], bias_far_recv.at[i], along(k))
        for i, k in enumerate(FAR)
    ]
    for copy in bias_far_copies:
        copy.start()

    arrived = got_far.at[pl.ds(0, 7)]
    pltpu.make_async_copy(arrived, arrived, far_recv).wait()
    final = got_far[0].astype(jnp.float32)
    for s in range(1, 8):
        final += got_far[s].astype(jnp.float32)
    final = (final * (1.0 / 128.0)).astype(jnp.bfloat16)
    tile[0] = final[:, :HD]
    tile[1] = final[:, HD:]

    target = weight_grad.at[y, c, xz, group]
    tile_copies = []
    for k in FAR + [0]:
        for h in range(2):
            there = pair * 2 + h
            copy = remote(tile.at[h], target, tile_send.at[len(tile_copies)], tile_recv.at[group],
                          at(x, there, (zq + k) % 8, zp, c))
            tile_copies.append((copy, k, there))
    own_tiles = [pltpu.make_async_copy(tile.at[h], target, tile_recv.at[group]) for h in range(2)]
    for copy, k, there in tile_copies:
        if k:
            copy.start()
        else:
            pl.when(there != y)(copy.start)
    for h in range(2):
        pl.when(pair * 2 + h == y)(own_tiles[h].start)

    load_weight.wait()
    for copy in weight_copies:
        copy.wait_recv()
    result = lax.dot_general(
        raw[...].reshape(2 * ROWS, HEADS * HD), weights[...],
        (((1,), (1,)), ((), ())), preferred_element_type=jnp.float32,
    )
    inputs[...] = result.astype(jnp.bfloat16).reshape(2, ROWS, HALF)
    input_copy = remote(inputs.at[other], input_grad.at[:, own_half], input_send, input_recv, sibling)
    input_copy.start()
    input_local = pltpu.make_async_copy(inputs.at[c], input_grad.at[:, own_half], input_own)
    input_local.start()

    arrivals = [group, (group + 1) % 4, (group + 3) % 4, (group + 2) % 4]
    wide_copies = []
    for j, g in enumerate(arrivals):
        block = weight_grad.at[:, c, xz, g]
        pltpu.make_async_copy(block, block, tile_recv.at[g]).wait()
        copies = [
            remote(block, block, wide_send.at[j, i], wide_recv.at[j, i], near(kx, kz))
            for i, (kx, kz) in enumerate(NEAR)
        ]
        for copy in copies:
            copy.start()
        wide_copies.append(copies)

    for copy in bias_far_copies:
        copy.wait()
    bias_all = bias_far[0]
    for s in range(1, 8):
        bias_all += bias_far[s]
    bias_grad[...] = bias_all[0:1] * (1.0 / 128.0)

    core_copies = []
    for j, g in enumerate(arrivals):
        for copy in wide_copies[j]:
            copy.wait_recv()
        block = weight_grad.at[:, c, :, g]
        copy = remote(block, block, core_send.at[j], core_recv.at[j], sibling)
        copy.start()
        core_copies.append(copy)

    for copy in raw_copies + [normed_copy] + sum(near_copies, []) + far_copies + weight_copies + sum(wide_copies, []):
        copy.wait_send()
    for copy, k, there in tile_copies:
        if k:
            copy.wait_send()
        else:
            pl.when(there != y)(copy.wait_send)
    input_copy.wait()
    input_local.wait()
    for copy in core_copies:
        copy.wait()


def finish(input_vmem, weight_vmem, bias_vmem, input_grad, weight_grad, bias_grad, done):
    copies = [
        pltpu.make_async_copy(weight_vmem, weight_grad, done.at[0]),
        pltpu.make_async_copy(input_vmem, input_grad, done.at[1]),
        pltpu.make_async_copy(bias_vmem, bias_grad, done.at[2]),
    ]
    for copy in copies:
        copy.start()
    for copy in copies:
        copy.wait()


def body(normed, key_weight, key_grad):
    dma, regular = pltpu.SemaphoreType.DMA, pltpu.SemaphoreType.REGULAR
    bf16, f32 = jnp.bfloat16, jnp.float32
    hbm = pl.BlockSpec(memory_space=pltpu.HBM)
    anywhere = pl.BlockSpec(memory_space=pl.ANY)
    local = pl.BlockSpec(memory_space=pltpu.VMEM)
    shapes = (
        jax.ShapeDtypeStruct((ROWS, WIDE), bf16),
        jax.ShapeDtypeStruct((4, 2, 8, GROUPS, 16, HD), bf16),
        jax.ShapeDtypeStruct((1, HD), f32),
    )
    normed, key_weight, key_grad = (pltpu.with_memory_space_constraint(a, pltpu.HBM) for a in (normed, key_weight, key_grad))
    results = pl.pallas_call(
        kernel,
        out_shape=shapes,
        in_specs=[hbm] * 3,
        out_specs=(anywhere, anywhere, local),
        scratch_shapes=[
            pltpu.VMEM((ROWS, HD), bf16),
            pltpu.VMEM((2, ROWS, HALF), bf16),
            pltpu.VMEM((HALF, 2 * ROWS), bf16),
            pltpu.VMEM((2, ROWS, HEADS * HD), bf16),
            pltpu.VMEM((HALF, HEADS * HD), bf16),
            pltpu.VMEM((8, GROUPS, 16, HEADS * HD), bf16),
            pltpu.VMEM((8, GROUPS, 16, HEADS * HD), bf16),
            pltpu.VMEM((8, 16, 2 * HD), bf16),
            pltpu.VMEM((8, 16, 2 * HD), bf16),
            pltpu.VMEM((2, 16, HD), bf16),
            pltpu.VMEM((2, ROWS, HALF), bf16),
            pltpu.VMEM((8, 8, HD), f32),
            pltpu.VMEM((8, 8, HD), f32),
            dma((3,)), dma((7,)), dma((7,)), dma, dma, dma((3,)), dma((3,)),
            dma((4, 7)), dma((4, 7)), dma((7,)), dma, dma((16,)), dma((4,)), dma((4, 7)), dma((4, 7)),
            dma((4,)), dma((4,)), dma, dma, dma,
            dma((7,)), dma((7,)), dma((7,)), dma((7,)), regular, regular,
        ],
        compiler_params=pltpu.CompilerParams(collective_id=0, has_side_effects=True, vmem_limit_bytes=32 << 20),
        cost_estimate=pl.CostEstimate(flops=4 * 256 * 512 * 512, bytes_accessed=4 << 20, transcendentals=0),
        name="key_projection_backward",
    )(normed, key_weight, key_grad)
    input_grad, weight_grad, bias_grad = pl.pallas_call(
        finish,
        out_shape=shapes,
        in_specs=[anywhere] * 3,
        out_specs=(hbm,) * 3,
        scratch_shapes=[dma((3,))],
        compiler_params=pltpu.CompilerParams(vmem_limit_bytes=1 << 20),
        name="write_results",
    )(*results)
    return input_grad, weight_grad.reshape(4096, HD), bias_grad.reshape(HD)


def solution(mesh):
    placed = (P(("dx", "dy"), "tp"), P(None, "tp"), P(("dx", "dy"), "tp"))
    return jax.shard_map(
        body,
        mesh=mesh,
        in_specs=placed,
        out_specs=(P(("dx", "dy"), "tp"), P(None, "tp"), P("tp")),
        check_vma=False,
    )
```

```python
import math

import jax
import jax.numpy as jnp
from jax import lax
from jax.experimental import pallas as pl
from jax.experimental.pallas import tpu as pltpu
from jax.sharding import PartitionSpec as P

HD = 128
SEQ = 4096
HEADS = 4
ROWS = 128
WIDE = 1024
HALF = 512
MESH = pl.DeviceIdType.MESH
NEAR = [(kx, kz) for kz in range(2) for kx in range(4) if (kx, kz) != (0, 0)]
NEAR.sort(key=lambda k: -(min(k[0], 4 - k[0]) + k[1]))
ACROSS = [(ky, kc) for ky in (2, 1, 3, 0) for kc in (1, 0) if (ky, kc) != (0, 0)]
FAR = [4, 3, 5, 2, 6, 1, 7]
GROUPS = 4


def rope_back(grad, first_row):
    values = grad.astype(jnp.float32)
    row = lax.broadcasted_iota(jnp.int32, (ROWS, HD), 0)
    lane = lax.broadcasted_iota(jnp.int32, (ROWS, HD), 1)
    positions = ((first_row + row) % SEQ).astype(jnp.float32)
    place = jnp.where(lane < HD // 2, lane, lane - HD // 2).astype(jnp.float32)
    angles = positions * jnp.exp(place * (-2.0 * math.log(1000000.0) / HD))
    sines = jnp.sin(angles)
    sines = jnp.where(lane < HD // 2, sines, -sines)
    return values * jnp.cos(angles) + pltpu.roll(values, HD // 2, 1) * sines


def split(row):
    high = row.astype(jnp.bfloat16).astype(jnp.float32)
    middle = (row - high).astype(jnp.bfloat16).astype(jnp.float32)
    place = lax.broadcasted_iota(jnp.int32, (16, HD), 0)
    low = jnp.where(place == 2, row - high - middle, 0.0)
    return jnp.where(place == 0, high, jnp.where(place == 1, middle, low)).astype(jnp.bfloat16)


def joined(tile):
    return tile[0:1] + tile[1:2] + tile[2:3]


def kernel(
    normed, key_weight, key_grad, input_grad, weight_grad, bias_grad,
    keys, tokens, turned, raw, weights, parts, got, halves, got_far, tile, inputs,
    load_sem, raw_send, raw_recv, normed_send, normed_recv, weight_send, weight_recv,
    near_send, near_recv, far_send, far_recv, tile_send, tile_recv, wide_send, wide_recv,
    core_send, core_recv, input_send, input_recv, input_own,
    cross_send, cross_recv, one_away, two_away,
):
    dx, dy, y = lax.axis_index("dx"), lax.axis_index("dy"), lax.axis_index("tp")
    x, c = dy % 4, dx % 2
    z = (dy // 4) * 8 + dx // 2
    zp, zq = z % 2, z // 2
    xz = x * 2 + zp
    group, pair = zq // 2, zq % 2
    other = 1 - c

    def at(x, y, zq, zp, c):
        z = zq * 2 + zp
        return ((z % 8) * 2 + c, (z // 8) * 4 + x, y)

    def along(k):
        return at(x, y, (zq + k) % 8, zp, c)

    def near(kx, kz):
        return at((x + kx) % 4, y, zq, (zp + kz) % 2, c)

    def signal(semaphore, device):
        pl.semaphore_signal(semaphore, inc=1, device_id=device, device_id_type=MESH)

    def remote(source, target, send, recv, device):
        return pltpu.make_async_remote_copy(
            src_ref=source, dst_ref=target, send_sem=send, recv_sem=recv, device_id=device, device_id_type=MESH
        )

    def wait_for(buffer, semaphore):
        pltpu.make_async_copy(buffer, buffer, semaphore).wait()

    sibling = at(x, y, zq, zp, other)
    barrier = pltpu.get_barrier_semaphore()
    partners = [along(1), along(7)] + [near(kx, kz) for kx, kz in NEAR]
    partners += [at(x, (y + ky) % 4, zq, zp, (c + kc) % 2) for ky, kc in ACROSS]
    for partner in partners:
        signal(barrier, partner)

    own_half = pl.ds(pl.multiple_of(c * HALF, HALF), HALF)
    other_half = pl.ds(pl.multiple_of(other * HALF, HALF), HALF)
    own_head = pl.ds(pl.multiple_of(y * HD, HD), HD)
    load_keys = pltpu.make_async_copy(key_grad, keys, load_sem.at[0])
    load_normed = pltpu.make_async_copy(normed.at[:, own_half], tokens.at[c], load_sem.at[1])
    own_rows = pl.ds(pl.multiple_of(y * WIDE + c * HALF, HALF), HALF)
    load_weight = pltpu.make_async_copy(key_weight.at[own_rows], weights.at[:, own_head], load_sem.at[2])
    load_keys.start()
    load_normed.start()
    load_weight.start()
    load_keys.wait()
    first_row = (dx * 8 + dy) * ROWS
    raw[c, :, own_head] = rope_back(keys[...], first_row).astype(jnp.bfloat16)

    pl.semaphore_wait(barrier, len(partners))

    raw_copies = [
        remote(raw.at[c, :, own_head], raw.at[c, :, own_head], raw_send.at[i], raw_recv.at[i],
               at(x, (y + ky) % 4, zq, zp, (c + kc) % 2))
        for i, (ky, kc) in enumerate(ACROSS)
    ]
    for copy in raw_copies:
        copy.start()
    normed_copy = remote(normed.at[:, other_half], tokens.at[c], normed_send, normed_recv, sibling)
    normed_copy.start()
    for k in (1, 7):
        signal(one_away, along(k))
    load_normed.wait()
    normed_copy.wait_recv()
    turned[...] = tokens[...].reshape(2 * ROWS, HALF).T
    pl.semaphore_wait(one_away, 2)
    for k in (2, 6):
        signal(two_away, along(k))
    for copy in raw_copies:
        copy.wait_recv()

    product = jnp.dot(
        turned[...], raw[...].reshape(2 * ROWS, HEADS * HD), preferred_element_type=jnp.float32
    )
    step = 1 + 2 * pair
    order = [(group + 2) % 4, (group + step) % 4, (group + 4 - step) % 4, group]
    main = pl.ds(0, HEADS * HD)
    parts[:, :, :, main] = product.astype(jnp.bfloat16).reshape(8, GROUPS, 16, HEADS * HD)
    raw_head = raw[:, :, own_head].astype(jnp.float32).reshape(2 * ROWS, HD)
    bias_part = split(jnp.sum(raw_head, axis=0, keepdims=True))
    for d in range(8):
        parts[d, order[0], :, HEADS * HD:] = bias_part
    near_copies = []
    for j, g in enumerate(order):
        lanes = pl.ds(0, HEADS * HD + HD) if j == 0 else main
        for kx, kz in NEAR:
            copy = remote(parts.at[((x + kx) % 4) * 2 + (zp + kz) % 2, g, :, lanes], got.at[xz, g, :, lanes],
                          near_send.at[j], near_recv.at[j], near(kx, kz))
            copy.start()
            near_copies.append(copy)
    got[xz] = parts[xz]

    pl.semaphore_wait(two_away, 2)
    far_copies = []
    for j, g in enumerate(order):
        lanes = pl.ds(0, HEADS * HD + HD) if j == 0 else main
        wait_for(got.at[pl.ds(0, 7), g, :, lanes], near_recv.at[j])
        total = got[0, g, :, lanes].astype(jnp.float32)
        for s in range(1, 8):
            total += got[s, g, :, lanes].astype(jnp.float32)
        if j == 0:
            bias_part = split(joined(total[:, HEADS * HD:]))
            for s in range(8):
                halves[s, :, 2 * HD:] = bias_part
        total = total.astype(jnp.bfloat16)
        for h in range(2):
            halves[g * 2 + h, :, :2 * HD] = total[:, h * 256:h * 256 + 256]
        for h in range(2 if j < 3 else 1):
            there = g * 2 + h if j < 3 else g * 2 + 1 - pair
            copy = remote(halves.at[there], got_far.at[zq], far_send, far_recv,
                          at(x, y, there, zp, c))
            copy.start()
            far_copies.append(copy)
    got_far[zq] = halves[zq]

    weight_copies = []
    for i, ky in enumerate((2, 1, 3)):
        there = (y + ky) % 4
        rows = pl.ds(pl.multiple_of(there * WIDE + c * HALF, HALF), HALF)
        weight_copies.append(
            remote(key_weight.at[rows], weights.at[:, own_head], weight_send.at[i], weight_recv.at[i],
                   at(x, there, zq, zp, c))
        )
    for copy in weight_copies:
        copy.start()

    wait_for(got_far.at[pl.ds(0, 7)], far_recv)
    final = got_far[0].astype(jnp.float32)
    for s in range(1, 8):
        final += got_far[s].astype(jnp.float32)
    bias_grad[...] = joined(final[:, 2 * HD:]) * (1.0 / 128.0)
    final = (final[:, :2 * HD] * (1.0 / 128.0)).astype(jnp.bfloat16)
    tile[0] = final[:, :HD]
    tile[1] = final[:, HD:]

    target = weight_grad.at[y, c, xz, group]
    tile_copies = []
    for k in FAR + [0]:
        for h in range(2):
            there = pair * 2 + h
            copy = remote(tile.at[h], target, tile_send.at[len(tile_copies)], tile_recv.at[group],
                          at(x, there, (zq + k) % 8, zp, c))
            tile_copies.append((copy, k, there))
    own_tiles = [pltpu.make_async_copy(tile.at[h], target, tile_recv.at[group]) for h in range(2)]
    for copy, k, there in tile_copies:
        if k:
            copy.start()
        else:
            pl.when(there != y)(copy.start)
    for h in range(2):
        pl.when(pair * 2 + h == y)(own_tiles[h].start)

    load_weight.wait()
    for copy in weight_copies:
        copy.wait_recv()
    result = lax.dot_general(
        raw[...].reshape(2 * ROWS, HEADS * HD), weights[...],
        (((1,), (1,)), ((), ())), preferred_element_type=jnp.float32,
    )
    inputs[...] = result.astype(jnp.bfloat16).reshape(2, ROWS, HALF)
    input_copy = remote(inputs.at[other], input_grad.at[:, own_half], input_send, input_recv, sibling)
    input_copy.start()
    input_local = pltpu.make_async_copy(inputs.at[c], input_grad.at[:, own_half], input_own)
    input_local.start()

    for copy in raw_copies + [normed_copy] + weight_copies:
        copy.wait_send()
    for j in range(GROUPS):
        lanes = pl.ds(0, HEADS * HD + HD) if j == 0 else main
        wait_for(parts.at[pl.ds(0, 7), 0, :, lanes], near_send.at[j])
    wait_for(halves.at[pl.ds(0, 7)], far_send)

    arrivals = [group, (group + 1) % 4, (group + 3) % 4, (group + 2) % 4]
    last = GROUPS - 1
    for j, g in enumerate(arrivals):
        block = weight_grad.at[:, c, xz, g]
        wait_for(block, tile_recv.at[g])
        for kx, kz in NEAR:
            if j == last:
                there = at((x + kx) % 4, y, zq, (zp + kz) % 2, other)
                remote(block, block, cross_send, cross_recv, there).start()
            remote(block, block, wide_send.at[j], wide_recv.at[j], near(kx, kz)).start()
        if j == last:
            remote(block, block, cross_send, cross_recv, sibling).start()
    for copy, k, there in tile_copies:
        if k:
            copy.wait_send()
        else:
            pl.when(there != y)(copy.wait_send)
    for j, g in enumerate(arrivals[:last]):
        wait_for(weight_grad.at[:, c, pl.ds(0, 7), g], wide_recv.at[j])
        block = weight_grad.at[:, c, :, g]
        remote(block, block, core_send.at[j], core_recv.at[j], sibling).start()
    for j, g in enumerate(arrivals):
        wait_for(weight_grad.at[:, c, pl.ds(0, 7), g], wide_send.at[j])
    input_copy.wait()
    input_local.wait()
    for j, g in enumerate(arrivals[:last]):
        wait_for(weight_grad.at[:, c, :, g], core_send.at[j])
        wait_for(weight_grad.at[:, other, :, g], core_recv.at[j])
    far = arrivals[last]
    wait_for(weight_grad.at[:, c, :, far], cross_send)
    wait_for(weight_grad.at[:, c, pl.ds(0, 7), far], wide_recv.at[last])
    wait_for(weight_grad.at[:, other, :, far], cross_recv)


def finish(input_vmem, weight_vmem, bias_vmem, input_grad, weight_grad, bias_grad, done):
    copies = [
        pltpu.make_async_copy(weight_vmem, weight_grad, done.at[0]),
        pltpu.make_async_copy(input_vmem, input_grad, done.at[1]),
        pltpu.make_async_copy(bias_vmem, bias_grad, done.at[2]),
    ]
    for copy in copies:
        copy.start()
    for copy in copies:
        copy.wait()


def body(normed, key_weight, key_grad):
    dma, regular = pltpu.SemaphoreType.DMA, pltpu.SemaphoreType.REGULAR
    bf16, f32 = jnp.bfloat16, jnp.float32
    hbm = pl.BlockSpec(memory_space=pltpu.HBM)
    anywhere = pl.BlockSpec(memory_space=pl.ANY)
    local = pl.BlockSpec(memory_space=pltpu.VMEM)
    shapes = (
        jax.ShapeDtypeStruct((ROWS, WIDE), bf16),
        jax.ShapeDtypeStruct((4, 2, 8, GROUPS, 16, HD), bf16),
        jax.ShapeDtypeStruct((1, HD), f32),
    )
    normed, key_weight, key_grad = (pltpu.with_memory_space_constraint(a, pltpu.HBM) for a in (normed, key_weight, key_grad))
    results = pl.pallas_call(
        kernel,
        out_shape=shapes,
        in_specs=[hbm] * 3,
        out_specs=(anywhere, anywhere, local),
        scratch_shapes=[
            pltpu.VMEM((ROWS, HD), bf16),
            pltpu.VMEM((2, ROWS, HALF), bf16),
            pltpu.VMEM((HALF, 2 * ROWS), bf16),
            pltpu.VMEM((2, ROWS, HEADS * HD), bf16),
            pltpu.VMEM((HALF, HEADS * HD), bf16),
            pltpu.VMEM((8, GROUPS, 16, HEADS * HD + HD), bf16),
            pltpu.VMEM((8, GROUPS, 16, HEADS * HD + HD), bf16),
            pltpu.VMEM((8, 16, 3 * HD), bf16),
            pltpu.VMEM((8, 16, 3 * HD), bf16),
            pltpu.VMEM((2, 16, HD), bf16),
            pltpu.VMEM((2, ROWS, HALF), bf16),
            dma((3,)), dma((7,)), dma((7,)), dma, dma, dma((3,)), dma((3,)),
            dma((4,)), dma((4,)), dma, dma, dma((16,)), dma((4,)), dma((4,)), dma((4,)),
            dma((3,)), dma((3,)), dma, dma, dma,
            dma, dma, regular, regular,
        ],
        compiler_params=pltpu.CompilerParams(collective_id=0, has_side_effects=True, vmem_limit_bytes=32 << 20),
        cost_estimate=pl.CostEstimate(flops=4 * 256 * 512 * 512, bytes_accessed=4 << 20, transcendentals=0),
        name="key_projection_backward",
    )(normed, key_weight, key_grad)
    input_grad, weight_grad, bias_grad = pl.pallas_call(
        finish,
        out_shape=shapes,
        in_specs=[anywhere] * 3,
        out_specs=(hbm,) * 3,
        scratch_shapes=[dma((3,))],
        compiler_params=pltpu.CompilerParams(vmem_limit_bytes=1 << 20),
        name="write_results",
    )(*results)
    return input_grad, weight_grad.reshape(4096, HD), bias_grad.reshape(HD)


def solution(mesh):
    placed = (P(("dx", "dy"), "tp"), P(None, "tp"), P(("dx", "dy"), "tp"))
    return jax.shard_map(
        body,
        mesh=mesh,
        in_specs=placed,
        out_specs=(P(("dx", "dy"), "tp"), P(None, "tp"), P("tp")),
        check_vma=False,
    )
```

```python
import math

import jax
import jax.numpy as jnp
from jax import lax
from jax.experimental import pallas as pl
from jax.experimental.pallas import tpu as pltpu
from jax.sharding import PartitionSpec as P

HD = 128
SEQ = 4096
HEADS = 4
ROWS = 128
WIDE = 1024
HALF = 512
MESH = pl.DeviceIdType.MESH
NEAR = [(kx, kz) for kz in range(2) for kx in range(4) if (kx, kz) != (0, 0)]
NEAR.sort(key=lambda k: -(min(k[0], 4 - k[0]) + k[1]))
ACROSS = [(ky, kc) for ky in (2, 1, 3, 0) for kc in (1, 0) if (ky, kc) != (0, 0)]
FAR = [4, 3, 5, 2, 6, 1, 7]
GROUPS = 4


def rope_back(grad, first_row):
    values = grad.astype(jnp.float32)
    row = lax.broadcasted_iota(jnp.int32, (ROWS, HD), 0)
    lane = lax.broadcasted_iota(jnp.int32, (ROWS, HD), 1)
    positions = ((first_row + row) % SEQ).astype(jnp.float32)
    place = jnp.where(lane < HD // 2, lane, lane - HD // 2).astype(jnp.float32)
    angles = positions * jnp.exp(place * (-2.0 * math.log(1000000.0) / HD))
    sines = jnp.sin(angles)
    sines = jnp.where(lane < HD // 2, sines, -sines)
    return values * jnp.cos(angles) + pltpu.roll(values, HD // 2, 1) * sines


def kernel(
    normed, key_weight, key_grad, input_grad, weight_grad, bias_grad,
    keys, tokens, turned, raw, weights, parts, got, halves, got_far, tile, inputs, bias_near, bias_far,
    load_sem, raw_send, raw_recv, normed_send, normed_recv, weight_send, weight_recv,
    near_send, near_recv, far_send, far_recv, tile_send, tile_recv, wide_send, wide_recv,
    core_send, core_recv, input_send, input_recv, input_own,
    cross_send, cross_recv, bias_send, bias_recv, one_away, two_away,
):
    dx, dy, y = lax.axis_index("dx"), lax.axis_index("dy"), lax.axis_index("tp")
    x, c = dy % 4, dx % 2
    z = (dy // 4) * 8 + dx // 2
    zp, zq = z % 2, z // 2
    xz = x * 2 + zp
    group, pair = zq // 2, zq % 2
    other = 1 - c

    def at(x, y, zq, zp, c):
        z = zq * 2 + zp
        return ((z % 8) * 2 + c, (z // 8) * 4 + x, y)

    def along(k):
        return at(x, y, (zq + k) % 8, zp, c)

    def near(kx, kz):
        return at((x + kx) % 4, y, zq, (zp + kz) % 2, c)

    def signal(semaphore, device):
        pl.semaphore_signal(semaphore, inc=1, device_id=device, device_id_type=MESH)

    def remote(source, target, send, recv, device):
        return pltpu.make_async_remote_copy(
            src_ref=source, dst_ref=target, send_sem=send, recv_sem=recv, device_id=device, device_id_type=MESH
        )

    def wait_for(buffer, semaphore):
        pltpu.make_async_copy(buffer, buffer, semaphore).wait()

    sibling = at(x, y, zq, zp, other)
    barrier = pltpu.get_barrier_semaphore()
    partners = [at(x, (y + ky) % 4, zq, zp, (c + kc) % 2) for ky, kc in ACROSS]
    partners += [near(kx, 0) for kx in (2, 1, 3)] + [near(0, 1), along(1), along(7)]
    partners += [at(x, y, (zq + k) % 8, 1 - zp, c) for k in (1, 7)]
    for partner in partners:
        signal(barrier, partner)

    own_half = pl.ds(pl.multiple_of(c * HALF, HALF), HALF)
    other_half = pl.ds(pl.multiple_of(other * HALF, HALF), HALF)
    own_head = pl.ds(pl.multiple_of(y * HD, HD), HD)
    load_keys = pltpu.make_async_copy(key_grad, keys, load_sem.at[0])
    load_normed = pltpu.make_async_copy(normed.at[:, own_half], tokens.at[c], load_sem.at[1])
    own_rows = pl.ds(pl.multiple_of(y * WIDE + c * HALF, HALF), HALF)
    load_weight = pltpu.make_async_copy(key_weight.at[own_rows], weights.at[:, own_head], load_sem.at[2])
    load_keys.start()
    load_normed.start()
    load_weight.start()
    load_keys.wait()
    first_row = (dx * 8 + dy) * ROWS
    raw[c, :, own_head] = rope_back(keys[...], first_row).astype(jnp.bfloat16)

    pl.semaphore_wait(barrier, len(partners))

    raw_copies = [
        remote(raw.at[c, :, own_head], raw.at[c, :, own_head], raw_send.at[i], raw_recv.at[i],
               at(x, (y + ky) % 4, zq, zp, (c + kc) % 2))
        for i, (ky, kc) in enumerate(ACROSS)
    ]
    for copy in raw_copies:
        copy.start()
    normed_copy = remote(normed.at[:, other_half], tokens.at[c], normed_send, normed_recv, sibling)
    normed_copy.start()
    for k in (1, 7):
        signal(one_away, along(k))
    load_normed.wait()
    normed_copy.wait_recv()
    turned[...] = tokens[...].reshape(2 * ROWS, HALF).T.reshape(8, GROUPS, 16, 2 * ROWS)
    pl.semaphore_wait(one_away, 2)
    for k in (2, 6):
        signal(two_away, along(k))
    raw_copies[-1].wait_recv()
    step = 1 + 2 * pair
    order = [(group + 2) % 4, (group + step) % 4, (group + 4 - step) % 4, group]
    raw_head = raw[:, :, own_head].astype(jnp.float32).reshape(2 * ROWS, HD)
    bias_near[x] = jnp.sum(raw_head, axis=0, keepdims=True)
    for copy in raw_copies[:-1]:
        copy.wait_recv()

    for j, g in enumerate(order):
        product = jnp.dot(
            turned[:, g].reshape(8 * 16, 2 * ROWS), raw[...].reshape(2 * ROWS, HEADS * HD),
            preferred_element_type=jnp.float32,
        )
        parts[:, g] = product.astype(jnp.bfloat16).reshape(8, 16, HEADS * HD)
        for kx in (2, 1, 3):
            remote(parts.at[pl.ds(((x + kx) % 4) * 2, 2), g], got.at[x, :, g],
                   near_send.at[j], near_recv.at[j], near(kx, 0)).start()
        if j == 0:
            for kx in (2, 1, 3):
                remote(bias_near.at[x], bias_near.at[x], bias_send.at[0], bias_recv.at[0], near(kx, 0)).start()
    got[x] = parts[pl.ds(x * 2, 2)]

    pl.semaphore_wait(two_away, 2)
    for j, g in enumerate(order):
        wait_for(got.at[pl.ds(0, 3), :, g], near_recv.at[j])
        total = got[0, :, g].astype(jnp.float32)
        for s in range(1, 4):
            total += got[s, :, g].astype(jnp.float32)
        total = total.astype(jnp.bfloat16)
        for h in range(2):
            for p in range(2):
                halves[(g * 2 + h) * 2 + p] = total[p, :, h * 256:h * 256 + 256]
        for h, p in ((pair, 1 - zp), (pair, zp), (1 - pair, zp), (1 - pair, 1 - zp)):
            if j == 3 and h is pair and p is zp:
                continue
            there = g * 2 + h
            remote(halves.at[there * 2 + p], got_far.at[z], far_send, far_recv, at(x, y, there, p, c)).start()
        if j == 0:
            wait_for(bias_near.at[pl.ds(0, 3)], bias_recv.at[0])
            bias_far[z] = bias_near[0] + bias_near[1] + bias_near[2] + bias_near[3]
            for k in (8, 7, 9, 6, 10, 5, 11, 4, 12, 3, 13, 2, 14, 1, 15):
                there = (z + k) % 16
                remote(bias_far.at[z], bias_far.at[z], bias_send.at[1], bias_recv.at[1],
                       at(x, y, there // 2, there % 2, c)).start()
    got_far[z] = halves[z]

    weight_copies = []
    for i, ky in enumerate((2, 1, 3)):
        there = (y + ky) % 4
        rows = pl.ds(pl.multiple_of(there * WIDE + c * HALF, HALF), HALF)
        weight_copies.append(
            remote(key_weight.at[rows], weights.at[:, own_head], weight_send.at[i], weight_recv.at[i],
                   at(x, there, zq, zp, c))
        )
    for copy in weight_copies:
        copy.start()

    wait_for(got_far.at[pl.ds(0, 15)], far_recv)
    final = got_far[0].astype(jnp.float32)
    for s in range(1, 16):
        final += got_far[s].astype(jnp.float32)
    final = (final * (1.0 / 128.0)).astype(jnp.bfloat16)
    tile[0] = final[:, :HD]
    tile[1] = final[:, HD:]

    target = weight_grad.at[y, c, xz, group]
    tile_copies = []
    for k in FAR + [0]:
        for h in range(2):
            there = pair * 2 + h
            copy = remote(tile.at[h], target, tile_send.at[len(tile_copies)], tile_recv.at[group],
                          at(x, there, (zq + k) % 8, zp, c))
            tile_copies.append((copy, k, there))
    own_tiles = [pltpu.make_async_copy(tile.at[h], target, tile_recv.at[group]) for h in range(2)]
    for copy, k, there in tile_copies:
        if k:
            copy.start()
        else:
            pl.when(there != y)(copy.start)
    for h in range(2):
        pl.when(pair * 2 + h == y)(own_tiles[h].start)

    wait_for(bias_far.at[pl.ds(0, 15)], bias_recv.at[1])
    bias_all = bias_far[0]
    for s in range(1, 16):
        bias_all += bias_far[s]
    bias_grad[...] = bias_all * (1.0 / 128.0)

    load_weight.wait()
    for copy in weight_copies:
        copy.wait_recv()
    result = lax.dot_general(
        raw[...].reshape(2 * ROWS, HEADS * HD), weights[...],
        (((1,), (1,)), ((), ())), preferred_element_type=jnp.float32,
    )
    inputs[...] = result.astype(jnp.bfloat16).reshape(2, ROWS, HALF)
    input_copy = remote(inputs.at[other], input_grad.at[:, own_half], input_send, input_recv, sibling)
    input_copy.start()
    input_local = pltpu.make_async_copy(inputs.at[c], input_grad.at[:, own_half], input_own)
    input_local.start()

    for copy in raw_copies + [normed_copy] + weight_copies:
        copy.wait_send()
    for j in range(GROUPS):
        wait_for(parts.at[pl.ds(0, 6), 0], near_send.at[j])
    wait_for(halves.at[pl.ds(0, 15)], far_send)
    wait_for(bias_near.at[pl.ds(0, 3)], bias_send.at[0])
    wait_for(bias_far.at[pl.ds(0, 15)], bias_send.at[1])

    arrivals = [group, (group + 1) % 4, (group + 3) % 4, (group + 2) % 4]
    last = GROUPS - 1
    for j, g in enumerate(arrivals):
        block = weight_grad.at[:, c, xz, g]
        wait_for(block, tile_recv.at[g])
        for kx, kz in NEAR:
            if j == last:
                there = at((x + kx) % 4, y, zq, (zp + kz) % 2, other)
                remote(block, block, cross_send, cross_recv, there).start()
            remote(block, block, wide_send.at[j], wide_recv.at[j], near(kx, kz)).start()
        if j == last:
            remote(block, block, cross_send, cross_recv, sibling).start()
    for copy, k, there in tile_copies:
        if k:
            copy.wait_send()
        else:
            pl.when(there != y)(copy.wait_send)
    for j, g in enumerate(arrivals[:last]):
        wait_for(weight_grad.at[:, c, pl.ds(0, 7), g], wide_recv.at[j])
        block = weight_grad.at[:, c, :, g]
        remote(block, block, core_send.at[j], core_recv.at[j], sibling).start()
    for j, g in enumerate(arrivals):
        wait_for(weight_grad.at[:, c, pl.ds(0, 7), g], wide_send.at[j])
    input_copy.wait()
    input_local.wait()
    for j, g in enumerate(arrivals[:last]):
        wait_for(weight_grad.at[:, c, :, g], core_send.at[j])
        wait_for(weight_grad.at[:, other, :, g], core_recv.at[j])
    far = arrivals[last]
    wait_for(weight_grad.at[:, c, :, far], cross_send)
    wait_for(weight_grad.at[:, c, pl.ds(0, 7), far], wide_recv.at[last])
    wait_for(weight_grad.at[:, other, :, far], cross_recv)


def finish(input_vmem, weight_vmem, bias_vmem, input_grad, weight_grad, bias_grad, done):
    copies = [
        pltpu.make_async_copy(weight_vmem, weight_grad, done.at[0]),
        pltpu.make_async_copy(input_vmem, input_grad, done.at[1]),
        pltpu.make_async_copy(bias_vmem, bias_grad, done.at[2]),
    ]
    for copy in copies:
        copy.start()
    for copy in copies:
        copy.wait()


def body(normed, key_weight, key_grad):
    dma, regular = pltpu.SemaphoreType.DMA, pltpu.SemaphoreType.REGULAR
    bf16, f32 = jnp.bfloat16, jnp.float32
    hbm = pl.BlockSpec(memory_space=pltpu.HBM)
    anywhere = pl.BlockSpec(memory_space=pl.ANY)
    local = pl.BlockSpec(memory_space=pltpu.VMEM)
    shapes = (
        jax.ShapeDtypeStruct((ROWS, WIDE), bf16),
        jax.ShapeDtypeStruct((4, 2, 8, GROUPS, 16, HD), bf16),
        jax.ShapeDtypeStruct((1, HD), f32),
    )
    normed, key_weight, key_grad = (pltpu.with_memory_space_constraint(a, pltpu.HBM) for a in (normed, key_weight, key_grad))
    results = pl.pallas_call(
        kernel,
        out_shape=shapes,
        in_specs=[hbm] * 3,
        out_specs=(anywhere, anywhere, local),
        scratch_shapes=[
            pltpu.VMEM((ROWS, HD), bf16),
            pltpu.VMEM((2, ROWS, HALF), bf16),
            pltpu.VMEM((8, GROUPS, 16, 2 * ROWS), bf16),
            pltpu.VMEM((2, ROWS, HEADS * HD), bf16),
            pltpu.VMEM((HALF, HEADS * HD), bf16),
            pltpu.VMEM((8, GROUPS, 16, HEADS * HD), bf16),
            pltpu.VMEM((4, 2, GROUPS, 16, HEADS * HD), bf16),
            pltpu.VMEM((16, 16, 2 * HD), bf16),
            pltpu.VMEM((16, 16, 2 * HD), bf16),
            pltpu.VMEM((2, 16, HD), bf16),
            pltpu.VMEM((2, ROWS, HALF), bf16),
            pltpu.VMEM((4, 1, HD), f32),
            pltpu.VMEM((16, 1, HD), f32),
            dma((3,)), dma((7,)), dma((7,)), dma, dma, dma((3,)), dma((3,)),
            dma((4,)), dma((4,)), dma, dma, dma((16,)), dma((4,)), dma((4,)), dma((4,)),
            dma((3,)), dma((3,)), dma, dma, dma,
            dma, dma, dma((2,)), dma((2,)), regular, regular,
        ],
        compiler_params=pltpu.CompilerParams(collective_id=0, has_side_effects=True, vmem_limit_bytes=32 << 20),
        cost_estimate=pl.CostEstimate(flops=4 * 256 * 512 * 512, bytes_accessed=4 << 20, transcendentals=0),
        name="key_projection_backward",
    )(normed, key_weight, key_grad)
    input_grad, weight_grad, bias_grad = pl.pallas_call(
        finish,
        out_shape=shapes,
        in_specs=[anywhere] * 3,
        out_specs=(hbm,) * 3,
        scratch_shapes=[dma((3,))],
        compiler_params=pltpu.CompilerParams(vmem_limit_bytes=1 << 20),
        name="write_results",
    )(*results)
    return input_grad, weight_grad.reshape(4096, HD), bias_grad.reshape(HD)


def solution(mesh):
    placed = (P(("dx", "dy"), "tp"), P(None, "tp"), P(("dx", "dy"), "tp"))
    return jax.shard_map(
        body,
        mesh=mesh,
        in_specs=placed,
        out_specs=(P(("dx", "dy"), "tp"), P(None, "tp"), P("tp")),
        check_vma=False,
    )
```

```python
import math

import jax
import jax.numpy as jnp
from jax import lax
from jax.experimental import pallas as pl
from jax.experimental.pallas import tpu as pltpu
from jax.sharding import PartitionSpec as P

HD = 128
SEQ = 4096
HEADS = 4
ROWS = 128
WIDE = 1024
HALF = 512
MESH = pl.DeviceIdType.MESH
NEAR = [(kx, kz) for kz in range(2) for kx in range(4) if (kx, kz) != (0, 0)]
NEAR.sort(key=lambda k: -(min(k[0], 4 - k[0]) + k[1]))
ACROSS = [(ky, kc) for ky in (2, 1, 3, 0) for kc in (1, 0) if (ky, kc) != (0, 0)]
FAR = [4, 3, 5, 2, 6, 1, 7]
GROUPS = 4


def rope_back(grad, first_row):
    values = grad.astype(jnp.float32)
    row = lax.broadcasted_iota(jnp.int32, (ROWS, HD), 0)
    lane = lax.broadcasted_iota(jnp.int32, (ROWS, HD), 1)
    positions = ((first_row + row) % SEQ).astype(jnp.float32)
    place = jnp.where(lane < HD // 2, lane, lane - HD // 2).astype(jnp.float32)
    angles = positions * jnp.exp(place * (-2.0 * math.log(1000000.0) / HD))
    sines = jnp.sin(angles)
    sines = jnp.where(lane < HD // 2, sines, -sines)
    return values * jnp.cos(angles) + pltpu.roll(values, HD // 2, 1) * sines


def kernel(
    normed, key_weight, key_grad, input_grad, weight_grad, bias_grad,
    keys, tokens, turned, raw, weights, parts, got, halves, got_far, tile, inputs, bias_near, bias_far,
    load_sem, raw_send, raw_recv, normed_send, normed_recv, weight_send, weight_recv,
    near_send, near_recv, far_send, far_recv, tile_send, tile_recv, wide_send, wide_recv,
    core_send, core_recv, input_send, input_recv, input_own,
    cross_send, cross_recv, bias_send, bias_recv, one_away, two_away,
):
    dx, dy, y = lax.axis_index("dx"), lax.axis_index("dy"), lax.axis_index("tp")
    x, c = dy % 4, dx % 2
    z = (dy // 4) * 8 + dx // 2
    zp, zq = z % 2, z // 2
    xz = x * 2 + zp
    group, pair = zq // 2, zq % 2
    other = 1 - c

    def at(x, y, zq, zp, c):
        z = zq * 2 + zp
        return ((z % 8) * 2 + c, (z // 8) * 4 + x, y)

    def along(k):
        return at(x, y, (zq + k) % 8, zp, c)

    def near(kx, kz):
        return at((x + kx) % 4, y, zq, (zp + kz) % 2, c)

    def signal(semaphore, device):
        pl.semaphore_signal(semaphore, inc=1, device_id=device, device_id_type=MESH)

    def remote(source, target, send, recv, device):
        return pltpu.make_async_remote_copy(
            src_ref=source, dst_ref=target, send_sem=send, recv_sem=recv, device_id=device, device_id_type=MESH
        )

    def wait_for(buffer, semaphore):
        pltpu.make_async_copy(buffer, buffer, semaphore).wait()

    sibling = at(x, y, zq, zp, other)
    barrier = pltpu.get_barrier_semaphore()
    partners = [at(x, (y + ky) % 4, zq, zp, (c + kc) % 2) for ky, kc in ACROSS]
    partners += [near(kx, 0) for kx in (2, 1, 3)] + [near(0, 1), along(1), along(7)]
    partners += [at(x, y, (zq + k) % 8, 1 - zp, c) for k in (1, 7)]
    for partner in partners:
        signal(barrier, partner)

    own_half = pl.ds(pl.multiple_of(c * HALF, HALF), HALF)
    other_half = pl.ds(pl.multiple_of(other * HALF, HALF), HALF)
    own_head = pl.ds(pl.multiple_of(y * HD, HD), HD)
    load_keys = pltpu.make_async_copy(key_grad, keys, load_sem.at[0])
    load_normed = pltpu.make_async_copy(normed.at[:, own_half], tokens.at[c], load_sem.at[1])
    own_rows = pl.ds(pl.multiple_of(y * WIDE + c * HALF, HALF), HALF)
    load_weight = pltpu.make_async_copy(key_weight.at[own_rows], weights.at[:, own_head], load_sem.at[2])
    load_keys.start()
    load_normed.start()
    load_weight.start()
    load_keys.wait()
    first_row = (dx * 8 + dy) * ROWS
    raw[c, :, own_head] = rope_back(keys[...], first_row).astype(jnp.bfloat16)

    pl.semaphore_wait(barrier, len(partners))

    raw_copies = [
        remote(raw.at[c, :, own_head], raw.at[c, :, own_head], raw_send.at[i], raw_recv.at[i],
               at(x, (y + ky) % 4, zq, zp, (c + kc) % 2))
        for i, (ky, kc) in enumerate(ACROSS)
    ]
    for copy in raw_copies:
        copy.start()
    normed_copy = remote(normed.at[:, other_half], tokens.at[c], normed_send, normed_recv, sibling)
    normed_copy.start()
    for k in (1, 7):
        signal(one_away, along(k))
    load_normed.wait()
    normed_copy.wait_recv()
    turned[...] = tokens[...].reshape(2 * ROWS, HALF).T.reshape(8, GROUPS, 16, 2 * ROWS)
    pl.semaphore_wait(one_away, 2)
    for k in (2, 6):
        signal(two_away, along(k))
    raw_copies[-1].wait_recv()
    step = 1 + 2 * pair
    order = [(group + 2) % 4, (group + step) % 4, (group + 4 - step) % 4, group]
    raw_head = raw[:, :, own_head].astype(jnp.float32).reshape(2 * ROWS, HD)
    bias_near[x] = jnp.sum(raw_head, axis=0, keepdims=True)
    for copy in raw_copies[:-1]:
        copy.wait_recv()

    first_columns = [pl.ds(pl.multiple_of(h * 2 * HD, 2 * HD), 2 * HD) for h in (pair, 1 - pair)]

    for j, g in enumerate(order):
        product = jnp.dot(
            turned[:, g].reshape(8 * 16, 2 * ROWS), raw[...].reshape(2 * ROWS, HEADS * HD),
            preferred_element_type=jnp.float32,
        )
        parts[:, g] = product.astype(jnp.bfloat16).reshape(8, 16, HEADS * HD)
        for h, columns in enumerate(first_columns if j == 0 else [pl.ds(0, HEADS * HD)]):
            i = h if j == 0 else j + 1
            for kx in (2, 1, 3):
                remote(parts.at[pl.ds(((x + kx) % 4) * 2, 2), g, :, columns], got.at[x, :, g, :, columns],
                       near_send.at[i], near_recv.at[i], near(kx, 0)).start()
        if j == 0:
            for kx in (2, 1, 3):
                remote(bias_near.at[x], bias_near.at[x], bias_send.at[0], bias_recv.at[0], near(kx, 0)).start()
    got[x] = parts[pl.ds(x * 2, 2)]

    pl.semaphore_wait(two_away, 2)
    for j, g in enumerate(order):
        if j == 0:
            for i, (h, columns) in enumerate(zip((pair, 1 - pair), first_columns)):
                wait_for(got.at[pl.ds(0, 3), :, g, :, columns], near_recv.at[i])
                total = got[0, :, g, :, columns].astype(jnp.float32)
                for s in range(1, 4):
                    total += got[s, :, g, :, columns].astype(jnp.float32)
                there = g * 2 + h
                halves[pl.ds(there * 2, 2)] = total.astype(jnp.bfloat16)
                for p in (1 - zp, zp):
                    remote(halves.at[there * 2 + p], got_far.at[z], far_send, far_recv, at(x, y, there, p, c)).start()
        else:
            wait_for(got.at[pl.ds(0, 3), :, g], near_recv.at[j + 1])
            total = got[0, :, g].astype(jnp.float32)
            for s in range(1, 4):
                total += got[s, :, g].astype(jnp.float32)
            total = total.astype(jnp.bfloat16)
            for h in range(2):
                halves[pl.ds((g * 2 + h) * 2, 2)] = total[:, :, h * 256:h * 256 + 256]
            for h, p in ((pair, 1 - zp), (pair, zp), (1 - pair, zp), (1 - pair, 1 - zp)):
                if j == 3 and h is pair and p is zp:
                    continue
                there = g * 2 + h
                remote(halves.at[there * 2 + p], got_far.at[z], far_send, far_recv, at(x, y, there, p, c)).start()
        if j == 0:
            wait_for(bias_near.at[pl.ds(0, 3)], bias_recv.at[0])
            bias_far[z] = bias_near[0] + bias_near[1] + bias_near[2] + bias_near[3]
            for k in (8, 7, 9, 6, 10, 5, 11, 4, 12, 3, 13, 2, 14, 1, 15):
                there = (z + k) % 16
                remote(bias_far.at[z], bias_far.at[z], bias_send.at[1], bias_recv.at[1],
                       at(x, y, there // 2, there % 2, c)).start()
    got_far[z] = halves[z]

    weight_copies = []
    for i, ky in enumerate((2, 1, 3)):
        there = (y + ky) % 4
        rows = pl.ds(pl.multiple_of(there * WIDE + c * HALF, HALF), HALF)
        weight_copies.append(
            remote(key_weight.at[rows], weights.at[:, own_head], weight_send.at[i], weight_recv.at[i],
                   at(x, there, zq, zp, c))
        )
    for copy in weight_copies:
        copy.start()

    wait_for(got_far.at[pl.ds(0, 15)], far_recv)
    final = got_far[0].astype(jnp.float32)
    for s in range(1, 16):
        final += got_far[s].astype(jnp.float32)
    final = (final * (1.0 / 128.0)).astype(jnp.bfloat16)
    tile[0] = final[:, :HD]
    tile[1] = final[:, HD:]

    target = weight_grad.at[y, c, xz, group]
    tile_copies = []
    for k in FAR + [0]:
        for h in range(2):
            there = pair * 2 + h
            copy = remote(tile.at[h], target, tile_send.at[len(tile_copies)], tile_recv.at[group],
                          at(x, there, (zq + k) % 8, zp, c))
            tile_copies.append((copy, k, there))
    own_tiles = [pltpu.make_async_copy(tile.at[h], target, tile_recv.at[group]) for h in range(2)]
    for copy, k, there in tile_copies:
        if k:
            copy.start()
        else:
            pl.when(there != y)(copy.start)
    for h in range(2):
        pl.when(pair * 2 + h == y)(own_tiles[h].start)

    wait_for(bias_far.at[pl.ds(0, 15)], bias_recv.at[1])
    bias_all = bias_far[0]
    for s in range(1, 16):
        bias_all += bias_far[s]
    bias_grad[...] = bias_all * (1.0 / 128.0)

    load_weight.wait()
    for copy in weight_copies:
        copy.wait_recv()
    result = lax.dot_general(
        raw[...].reshape(2 * ROWS, HEADS * HD), weights[...],
        (((1,), (1,)), ((), ())), preferred_element_type=jnp.float32,
    )
    inputs[...] = result.astype(jnp.bfloat16).reshape(2, ROWS, HALF)
    input_copy = remote(inputs.at[other], input_grad.at[:, own_half], input_send, input_recv, sibling)
    input_copy.start()
    input_local = pltpu.make_async_copy(inputs.at[c], input_grad.at[:, own_half], input_own)
    input_local.start()

    for copy in raw_copies + [normed_copy] + weight_copies:
        copy.wait_send()
    for i in range(2):
        wait_for(parts.at[pl.ds(0, 6), 0, :, first_columns[i]], near_send.at[i])
    for j in range(1, GROUPS):
        wait_for(parts.at[pl.ds(0, 6), 0], near_send.at[j + 1])
    wait_for(halves.at[pl.ds(0, 15)], far_send)
    wait_for(bias_near.at[pl.ds(0, 3)], bias_send.at[0])
    wait_for(bias_far.at[pl.ds(0, 15)], bias_send.at[1])

    arrivals = [group, (group + 4 - step) % 4, (group + step) % 4, (group + 2) % 4]
    last = GROUPS - 1
    for j, g in enumerate(arrivals):
        block = weight_grad.at[:, c, xz, g]
        wait_for(block, tile_recv.at[g])
        for kx, kz in NEAR:
            if j == last:
                there = at((x + kx) % 4, y, zq, (zp + kz) % 2, other)
                remote(block, block, cross_send, cross_recv, there).start()
            remote(block, block, wide_send.at[j], wide_recv.at[j], near(kx, kz)).start()
        if j == last:
            remote(block, block, cross_send, cross_recv, sibling).start()
    for copy, k, there in tile_copies:
        if k:
            copy.wait_send()
        else:
            pl.when(there != y)(copy.wait_send)
    for j, g in enumerate(arrivals[:last]):
        wait_for(weight_grad.at[:, c, pl.ds(0, 7), g], wide_recv.at[j])
        block = weight_grad.at[:, c, :, g]
        remote(block, block, core_send.at[j], core_recv.at[j], sibling).start()
    for j, g in enumerate(arrivals):
        wait_for(weight_grad.at[:, c, pl.ds(0, 7), g], wide_send.at[j])
    input_copy.wait()
    input_local.wait()
    for j, g in enumerate(arrivals[:last]):
        wait_for(weight_grad.at[:, c, :, g], core_send.at[j])
        wait_for(weight_grad.at[:, other, :, g], core_recv.at[j])
    far = arrivals[last]
    wait_for(weight_grad.at[:, c, :, far], cross_send)
    wait_for(weight_grad.at[:, c, pl.ds(0, 7), far], wide_recv.at[last])
    wait_for(weight_grad.at[:, other, :, far], cross_recv)


def finish(input_vmem, weight_vmem, bias_vmem, input_grad, weight_grad, bias_grad, done):
    copies = [
        pltpu.make_async_copy(weight_vmem, weight_grad, done.at[0]),
        pltpu.make_async_copy(input_vmem, input_grad, done.at[1]),
        pltpu.make_async_copy(bias_vmem, bias_grad, done.at[2]),
    ]
    for copy in copies:
        copy.start()
    for copy in copies:
        copy.wait()


def body(normed, key_weight, key_grad):
    dma, regular = pltpu.SemaphoreType.DMA, pltpu.SemaphoreType.REGULAR
    bf16, f32 = jnp.bfloat16, jnp.float32
    hbm = pl.BlockSpec(memory_space=pltpu.HBM)
    anywhere = pl.BlockSpec(memory_space=pl.ANY)
    local = pl.BlockSpec(memory_space=pltpu.VMEM)
    shapes = (
        jax.ShapeDtypeStruct((ROWS, WIDE), bf16),
        jax.ShapeDtypeStruct((4, 2, 8, GROUPS, 16, HD), bf16),
        jax.ShapeDtypeStruct((1, HD), f32),
    )
    normed, key_weight, key_grad = (pltpu.with_memory_space_constraint(a, pltpu.HBM) for a in (normed, key_weight, key_grad))
    results = pl.pallas_call(
        kernel,
        out_shape=shapes,
        in_specs=[hbm] * 3,
        out_specs=(anywhere, anywhere, local),
        scratch_shapes=[
            pltpu.VMEM((ROWS, HD), bf16),
            pltpu.VMEM((2, ROWS, HALF), bf16),
            pltpu.VMEM((8, GROUPS, 16, 2 * ROWS), bf16),
            pltpu.VMEM((2, ROWS, HEADS * HD), bf16),
            pltpu.VMEM((HALF, HEADS * HD), bf16),
            pltpu.VMEM((8, GROUPS, 16, HEADS * HD), bf16),
            pltpu.VMEM((4, 2, GROUPS, 16, HEADS * HD), bf16),
            pltpu.VMEM((16, 16, 2 * HD), bf16),
            pltpu.VMEM((16, 16, 2 * HD), bf16),
            pltpu.VMEM((2, 16, HD), bf16),
            pltpu.VMEM((2, ROWS, HALF), bf16),
            pltpu.VMEM((4, 1, HD), f32),
            pltpu.VMEM((16, 1, HD), f32),
            dma((3,)), dma((7,)), dma((7,)), dma, dma, dma((3,)), dma((3,)),
            dma((5,)), dma((5,)), dma, dma, dma((16,)), dma((4,)), dma((4,)), dma((4,)),
            dma((3,)), dma((3,)), dma, dma, dma,
            dma, dma, dma((2,)), dma((2,)), regular, regular,
        ],
        compiler_params=pltpu.CompilerParams(collective_id=0, has_side_effects=True, vmem_limit_bytes=32 << 20),
        cost_estimate=pl.CostEstimate(flops=4 * 256 * 512 * 512, bytes_accessed=4 << 20, transcendentals=0),
        name="key_projection_backward",
    )(normed, key_weight, key_grad)
    input_grad, weight_grad, bias_grad = pl.pallas_call(
        finish,
        out_shape=shapes,
        in_specs=[anywhere] * 3,
        out_specs=(hbm,) * 3,
        scratch_shapes=[dma((3,))],
        compiler_params=pltpu.CompilerParams(vmem_limit_bytes=1 << 20),
        name="write_results",
    )(*results)
    return input_grad, weight_grad.reshape(4096, HD), bias_grad.reshape(HD)


def solution(mesh):
    placed = (P(("dx", "dy"), "tp"), P(None, "tp"), P(("dx", "dy"), "tp"))
    return jax.shard_map(
        body,
        mesh=mesh,
        in_specs=placed,
        out_specs=(P(("dx", "dy"), "tp"), P(None, "tp"), P("tp")),
        check_vma=False,
    )
```

```python
import math

import jax
import jax.numpy as jnp
from jax import lax
from jax.experimental import pallas as pl
from jax.experimental.pallas import tpu as pltpu
from jax.sharding import PartitionSpec as P

HD = 128
SEQ = 4096
HEADS = 4
ROWS = 128
WIDE = 1024
HALF = 512
MESH = pl.DeviceIdType.MESH
NEAR = [(kx, kz) for kz in range(2) for kx in range(4) if (kx, kz) != (0, 0)]
NEAR.sort(key=lambda k: -(min(k[0], 4 - k[0]) + k[1]))
ACROSS = [(ky, kc) for ky in (2, 1, 3, 0) for kc in (1, 0) if (ky, kc) != (0, 0)]
FAR = [4, 3, 5, 2, 6, 1, 7]
GROUPS = 4


def rope_back(grad, first_row):
    values = grad.astype(jnp.float32)
    row = lax.broadcasted_iota(jnp.int32, (ROWS, HD), 0)
    lane = lax.broadcasted_iota(jnp.int32, (ROWS, HD), 1)
    positions = ((first_row + row) % SEQ).astype(jnp.float32)
    place = jnp.where(lane < HD // 2, lane, lane - HD // 2).astype(jnp.float32)
    angles = positions * jnp.exp(place * (-2.0 * math.log(1000000.0) / HD))
    sines = jnp.sin(angles)
    sines = jnp.where(lane < HD // 2, sines, -sines)
    return values * jnp.cos(angles) + pltpu.roll(values, HD // 2, 1) * sines


def kernel(
    normed, key_weight, key_grad, input_grad, weight_grad, bias_grad,
    keys, tokens, turned, raw, weights, parts, got, halves, got_far, tile, inputs, bias_near, bias_far,
    load_sem, raw_send, raw_recv, normed_send, normed_recv, weight_send, weight_recv,
    near_send, near_recv, far_send, far_recv, tile_send, tile_recv, wide_send, wide_recv,
    core_send, core_recv, input_send, input_recv, input_own,
    cross_send, cross_recv, bias_send, bias_recv, one_away, two_away,
):
    dx, dy, y = lax.axis_index("dx"), lax.axis_index("dy"), lax.axis_index("tp")
    x, c = dy % 4, dx % 2
    z = (dy // 4) * 8 + dx // 2
    zp, zq = z % 2, z // 2
    xz = x * 2 + zp
    group, pair = zq // 2, zq % 2
    other = 1 - c

    def at(x, y, zq, zp, c):
        z = zq * 2 + zp
        return ((z % 8) * 2 + c, (z // 8) * 4 + x, y)

    def along(k):
        return at(x, y, (zq + k) % 8, zp, c)

    def near(kx, kz):
        return at((x + kx) % 4, y, zq, (zp + kz) % 2, c)

    def signal(semaphore, device):
        pl.semaphore_signal(semaphore, inc=1, device_id=device, device_id_type=MESH)

    def remote(source, target, send, recv, device):
        return pltpu.make_async_remote_copy(
            src_ref=source, dst_ref=target, send_sem=send, recv_sem=recv, device_id=device, device_id_type=MESH
        )

    def wait_for(buffer, semaphore):
        pltpu.make_async_copy(buffer, buffer, semaphore).wait()

    sibling = at(x, y, zq, zp, other)
    barrier = pltpu.get_barrier_semaphore()
    partners = [at(x, (y + ky) % 4, zq, zp, (c + kc) % 2) for ky, kc in ACROSS]
    partners += [near(kx, 0) for kx in (2, 1, 3)] + [near(0, 1), along(1), along(7)]
    partners += [at(x, y, (zq + k) % 8, 1 - zp, c) for k in (1, 7)]
    for partner in partners:
        signal(barrier, partner)

    own_half = pl.ds(pl.multiple_of(c * HALF, HALF), HALF)
    other_half = pl.ds(pl.multiple_of(other * HALF, HALF), HALF)
    own_head = pl.ds(pl.multiple_of(y * HD, HD), HD)
    load_keys = pltpu.make_async_copy(key_grad, keys, load_sem.at[0])
    load_normed = pltpu.make_async_copy(normed.at[:, own_half], tokens.at[c], load_sem.at[1])
    own_rows = pl.ds(pl.multiple_of(y * WIDE + c * HALF, HALF), HALF)
    load_weight = pltpu.make_async_copy(key_weight.at[own_rows], weights.at[:, own_head], load_sem.at[2])
    load_keys.start()
    load_normed.start()
    load_weight.start()
    load_keys.wait()
    first_row = (dx * 8 + dy) * ROWS
    raw[c, :, own_head] = rope_back(keys[...], first_row).astype(jnp.bfloat16)

    pl.semaphore_wait(barrier, len(partners))

    raw_copies = [
        remote(raw.at[c, :, own_head], raw.at[c, :, own_head], raw_send.at[i], raw_recv.at[i],
               at(x, (y + ky) % 4, zq, zp, (c + kc) % 2))
        for i, (ky, kc) in enumerate(ACROSS)
    ]
    for copy in raw_copies:
        copy.start()
    normed_copy = remote(normed.at[:, other_half], tokens.at[c], normed_send, normed_recv, sibling)
    normed_copy.start()
    for k in (1, 7):
        signal(one_away, along(k))
    load_normed.wait()
    normed_copy.wait_recv()
    turned[...] = tokens[...].reshape(2 * ROWS, HALF).T.reshape(8, GROUPS, 16, 2 * ROWS)
    pl.semaphore_wait(one_away, 2)
    for k in (2, 6):
        signal(two_away, along(k))
    raw_copies[-1].wait_recv()
    step = 1 + 2 * pair
    order = [(group + 2) % 4, (group + step) % 4, (group + 4 - step) % 4, group]
    raw_head = raw[:, :, own_head].astype(jnp.float32).reshape(2 * ROWS, HD)
    bias_near[x] = jnp.sum(raw_head, axis=0, keepdims=True)
    for copy in raw_copies[:-1]:
        copy.wait_recv()

    farther = [(pair, 1 - pair), (1 - pair, pair)]
    columns_of = [[pl.ds(pl.multiple_of(h * 2 * HD, 2 * HD), 2 * HD) for h in both] for both in farther]

    for j, g in enumerate(order):
        product = jnp.dot(
            turned[:, g].reshape(8 * 16, 2 * ROWS), raw[...].reshape(2 * ROWS, HEADS * HD),
            preferred_element_type=jnp.float32,
        )
        parts[:, g] = product.astype(jnp.bfloat16).reshape(8, 16, HEADS * HD)
        for h, columns in enumerate(columns_of[j] if j < 2 else [pl.ds(0, HEADS * HD)]):
            i = j * 2 + h if j < 2 else j + 2
            for kx in (2, 1, 3):
                remote(parts.at[pl.ds(((x + kx) % 4) * 2, 2), g, :, columns], got.at[x, :, g, :, columns],
                       near_send.at[i], near_recv.at[i], near(kx, 0)).start()
        if j == 0:
            for kx in (2, 1, 3):
                remote(bias_near.at[x], bias_near.at[x], bias_send.at[0], bias_recv.at[0], near(kx, 0)).start()
    got[x] = parts[pl.ds(x * 2, 2)]

    pl.semaphore_wait(two_away, 2)
    for j, g in enumerate(order):
        if j < 2:
            for i, (h, columns) in enumerate(zip(farther[j], columns_of[j])):
                wait_for(got.at[pl.ds(0, 3), :, g, :, columns], near_recv.at[j * 2 + i])
                total = got[0, :, g, :, columns].astype(jnp.float32)
                for s in range(1, 4):
                    total += got[s, :, g, :, columns].astype(jnp.float32)
                there = g * 2 + h
                halves[pl.ds(there * 2, 2)] = total.astype(jnp.bfloat16)
                for p in (1 - zp, zp):
                    remote(halves.at[there * 2 + p], got_far.at[z], far_send, far_recv, at(x, y, there, p, c)).start()
        else:
            wait_for(got.at[pl.ds(0, 3), :, g], near_recv.at[j + 2])
            total = got[0, :, g].astype(jnp.float32)
            for s in range(1, 4):
                total += got[s, :, g].astype(jnp.float32)
            total = total.astype(jnp.bfloat16)
            for h in range(2):
                halves[pl.ds((g * 2 + h) * 2, 2)] = total[:, :, h * 256:h * 256 + 256]
            for h, p in ((pair, 1 - zp), (pair, zp), (1 - pair, zp), (1 - pair, 1 - zp)):
                if j == 3 and h is pair and p is zp:
                    continue
                there = g * 2 + h
                remote(halves.at[there * 2 + p], got_far.at[z], far_send, far_recv, at(x, y, there, p, c)).start()
        if j == 0:
            wait_for(bias_near.at[pl.ds(0, 3)], bias_recv.at[0])
            bias_far[z] = bias_near[0] + bias_near[1] + bias_near[2] + bias_near[3]
            for k in (8, 7, 9, 6, 10, 5, 11, 4, 12, 3, 13, 2, 14, 1, 15):
                there = (z + k) % 16
                remote(bias_far.at[z], bias_far.at[z], bias_send.at[1], bias_recv.at[1],
                       at(x, y, there // 2, there % 2, c)).start()
    got_far[z] = halves[z]

    weight_copies = []
    for i, ky in enumerate((2, 1, 3)):
        there = (y + ky) % 4
        rows = pl.ds(pl.multiple_of(there * WIDE + c * HALF, HALF), HALF)
        weight_copies.append(
            remote(key_weight.at[rows], weights.at[:, own_head], weight_send.at[i], weight_recv.at[i],
                   at(x, there, zq, zp, c))
        )
    for copy in weight_copies:
        copy.start()

    wait_for(got_far.at[pl.ds(0, 15)], far_recv)
    final = got_far[0].astype(jnp.float32)
    for s in range(1, 16):
        final += got_far[s].astype(jnp.float32)
    final = (final * (1.0 / 128.0)).astype(jnp.bfloat16)
    tile[0] = final[:, :HD]
    tile[1] = final[:, HD:]

    target = weight_grad.at[y, c, xz, group]
    tile_copies = []
    for k in FAR + [0]:
        for h in range(2):
            there = pair * 2 + h
            copy = remote(tile.at[h], target, tile_send.at[len(tile_copies)], tile_recv.at[group],
                          at(x, there, (zq + k) % 8, zp, c))
            tile_copies.append((copy, k, there))
    own_tiles = [pltpu.make_async_copy(tile.at[h], target, tile_recv.at[group]) for h in range(2)]
    for copy, k, there in tile_copies:
        if k:
            copy.start()
        else:
            pl.when(there != y)(copy.start)
    for h in range(2):
        pl.when(pair * 2 + h == y)(own_tiles[h].start)

    wait_for(bias_far.at[pl.ds(0, 15)], bias_recv.at[1])
    bias_all = bias_far[0]
    for s in range(1, 16):
        bias_all += bias_far[s]
    bias_grad[...] = bias_all * (1.0 / 128.0)

    load_weight.wait()
    for copy in weight_copies:
        copy.wait_recv()
    result = lax.dot_general(
        raw[...].reshape(2 * ROWS, HEADS * HD), weights[...],
        (((1,), (1,)), ((), ())), preferred_element_type=jnp.float32,
    )
    inputs[...] = result.astype(jnp.bfloat16).reshape(2, ROWS, HALF)
    input_copy = remote(inputs.at[other], input_grad.at[:, own_half], input_send, input_recv, sibling)
    input_copy.start()
    input_local = pltpu.make_async_copy(inputs.at[c], input_grad.at[:, own_half], input_own)
    input_local.start()

    for copy in raw_copies + [normed_copy] + weight_copies:
        copy.wait_send()
    for i in range(4):
        wait_for(parts.at[pl.ds(0, 6), 0, :, pl.ds(0, 2 * HD)], near_send.at[i])
    for j in range(2, GROUPS):
        wait_for(parts.at[pl.ds(0, 6), 0], near_send.at[j + 2])
    wait_for(halves.at[pl.ds(0, 15)], far_send)
    wait_for(bias_near.at[pl.ds(0, 3)], bias_send.at[0])
    wait_for(bias_far.at[pl.ds(0, 15)], bias_send.at[1])

    arrivals = [group, (group + 4 - step) % 4, (group + step) % 4, (group + 2) % 4]
    last = GROUPS - 1
    for j, g in enumerate(arrivals):
        block = weight_grad.at[:, c, xz, g]
        wait_for(block, tile_recv.at[g])
        for kx, kz in NEAR:
            if j == last:
                there = at((x + kx) % 4, y, zq, (zp + kz) % 2, other)
                remote(block, block, cross_send, cross_recv, there).start()
            remote(block, block, wide_send.at[j], wide_recv.at[j], near(kx, kz)).start()
        if j == last:
            remote(block, block, cross_send, cross_recv, sibling).start()
    for copy, k, there in tile_copies:
        if k:
            copy.wait_send()
        else:
            pl.when(there != y)(copy.wait_send)
    for j, g in enumerate(arrivals[:last]):
        wait_for(weight_grad.at[:, c, pl.ds(0, 7), g], wide_recv.at[j])
        block = weight_grad.at[:, c, :, g]
        remote(block, block, core_send.at[j], core_recv.at[j], sibling).start()
    for j, g in enumerate(arrivals):
        wait_for(weight_grad.at[:, c, pl.ds(0, 7), g], wide_send.at[j])
    input_copy.wait()
    input_local.wait()
    for j, g in enumerate(arrivals[:last]):
        wait_for(weight_grad.at[:, c, :, g], core_send.at[j])
        wait_for(weight_grad.at[:, other, :, g], core_recv.at[j])
    far = arrivals[last]
    wait_for(weight_grad.at[:, c, :, far], cross_send)
    wait_for(weight_grad.at[:, c, pl.ds(0, 7), far], wide_recv.at[last])
    wait_for(weight_grad.at[:, other, :, far], cross_recv)


def finish(input_vmem, weight_vmem, bias_vmem, input_grad, weight_grad, bias_grad, done):
    copies = [
        pltpu.make_async_copy(weight_vmem, weight_grad, done.at[0]),
        pltpu.make_async_copy(input_vmem, input_grad, done.at[1]),
        pltpu.make_async_copy(bias_vmem, bias_grad, done.at[2]),
    ]
    for copy in copies:
        copy.start()
    for copy in copies:
        copy.wait()


def body(normed, key_weight, key_grad):
    dma, regular = pltpu.SemaphoreType.DMA, pltpu.SemaphoreType.REGULAR
    bf16, f32 = jnp.bfloat16, jnp.float32
    hbm = pl.BlockSpec(memory_space=pltpu.HBM)
    anywhere = pl.BlockSpec(memory_space=pl.ANY)
    local = pl.BlockSpec(memory_space=pltpu.VMEM)
    shapes = (
        jax.ShapeDtypeStruct((ROWS, WIDE), bf16),
        jax.ShapeDtypeStruct((4, 2, 8, GROUPS, 16, HD), bf16),
        jax.ShapeDtypeStruct((1, HD), f32),
    )
    normed, key_weight, key_grad = (pltpu.with_memory_space_constraint(a, pltpu.HBM) for a in (normed, key_weight, key_grad))
    results = pl.pallas_call(
        kernel,
        out_shape=shapes,
        in_specs=[hbm] * 3,
        out_specs=(anywhere, anywhere, local),
        scratch_shapes=[
            pltpu.VMEM((ROWS, HD), bf16),
            pltpu.VMEM((2, ROWS, HALF), bf16),
            pltpu.VMEM((8, GROUPS, 16, 2 * ROWS), bf16),
            pltpu.VMEM((2, ROWS, HEADS * HD), bf16),
            pltpu.VMEM((HALF, HEADS * HD), bf16),
            pltpu.VMEM((8, GROUPS, 16, HEADS * HD), bf16),
            pltpu.VMEM((4, 2, GROUPS, 16, HEADS * HD), bf16),
            pltpu.VMEM((16, 16, 2 * HD), bf16),
            pltpu.VMEM((16, 16, 2 * HD), bf16),
            pltpu.VMEM((2, 16, HD), bf16),
            pltpu.VMEM((2, ROWS, HALF), bf16),
            pltpu.VMEM((4, 1, HD), f32),
            pltpu.VMEM((16, 1, HD), f32),
            dma((3,)), dma((7,)), dma((7,)), dma, dma, dma((3,)), dma((3,)),
            dma((6,)), dma((6,)), dma, dma, dma((16,)), dma((4,)), dma((4,)), dma((4,)),
            dma((3,)), dma((3,)), dma, dma, dma,
            dma, dma, dma((2,)), dma((2,)), regular, regular,
        ],
        compiler_params=pltpu.CompilerParams(collective_id=0, has_side_effects=True, vmem_limit_bytes=32 << 20),
        cost_estimate=pl.CostEstimate(flops=4 * 256 * 512 * 512, bytes_accessed=4 << 20, transcendentals=0),
        name="key_projection_backward",
    )(normed, key_weight, key_grad)
    input_grad, weight_grad, bias_grad = pl.pallas_call(
        finish,
        out_shape=shapes,
        in_specs=[anywhere] * 3,
        out_specs=(hbm,) * 3,
        scratch_shapes=[dma((3,))],
        compiler_params=pltpu.CompilerParams(vmem_limit_bytes=1 << 20),
        name="write_results",
    )(*results)
    return input_grad, weight_grad.reshape(4096, HD), bias_grad.reshape(HD)


def solution(mesh):
    placed = (P(("dx", "dy"), "tp"), P(None, "tp"), P(("dx", "dy"), "tp"))
    return jax.shard_map(
        body,
        mesh=mesh,
        in_specs=placed,
        out_specs=(P(("dx", "dy"), "tp"), P(None, "tp"), P("tp")),
        check_vma=False,
    )
```

```python
import math

import jax
import jax.numpy as jnp
from jax import lax
from jax.experimental import pallas as pl
from jax.experimental.pallas import tpu as pltpu
from jax.sharding import PartitionSpec as P

HD = 128
SEQ = 4096
HEADS = 4
ROWS = 128
WIDE = 1024
HALF = 512
MESH = pl.DeviceIdType.MESH
NEAR = [(kx, kz) for kz in range(2) for kx in range(4) if (kx, kz) != (0, 0)]
NEAR.sort(key=lambda k: -(min(k[0], 4 - k[0]) + k[1]))
ACROSS = [(ky, kc) for ky in (2, 1, 3, 0) for kc in (1, 0) if (ky, kc) != (0, 0)]
FAR = [4, 3, 5, 2, 6, 1, 7]
GROUPS = 4


def rope_back(grad, first_row):
    values = grad.astype(jnp.float32)
    row = lax.broadcasted_iota(jnp.int32, (ROWS, HD), 0)
    lane = lax.broadcasted_iota(jnp.int32, (ROWS, HD), 1)
    positions = ((first_row + row) % SEQ).astype(jnp.float32)
    place = jnp.where(lane < HD // 2, lane, lane - HD // 2).astype(jnp.float32)
    angles = positions * jnp.exp(place * (-2.0 * math.log(1000000.0) / HD))
    sines = jnp.sin(angles)
    sines = jnp.where(lane < HD // 2, sines, -sines)
    return values * jnp.cos(angles) + pltpu.roll(values, HD // 2, 1) * sines


def kernel(
    normed, key_weight, key_grad, input_grad, weight_grad, bias_grad,
    keys, tokens, turned, raw, weights, parts, got, halves, got_far, tile, inputs, bias_near, bias_far,
    load_sem, raw_send, raw_recv, normed_send, normed_recv, weight_send, weight_recv,
    near_send, near_recv, far_send, far_recv, tile_send, tile_recv, wide_send, wide_recv,
    core_send, core_recv, input_send, input_recv, input_own,
    cross_send, cross_recv, bias_send, bias_recv, one_away, two_away,
):
    dx, dy, y = lax.axis_index("dx"), lax.axis_index("dy"), lax.axis_index("tp")
    x, c = dy % 4, dx % 2
    z = (dy // 4) * 8 + dx // 2
    zp, zq = z % 2, z // 2
    xz = x * 2 + zp
    group, pair = zq // 2, zq % 2
    other = 1 - c

    def at(x, y, zq, zp, c):
        z = zq * 2 + zp
        return ((z % 8) * 2 + c, (z // 8) * 4 + x, y)

    def along(k):
        return at(x, y, (zq + k) % 8, zp, c)

    def near(kx, kz):
        return at((x + kx) % 4, y, zq, (zp + kz) % 2, c)

    def signal(semaphore, device):
        pl.semaphore_signal(semaphore, inc=1, device_id=device, device_id_type=MESH)

    def remote(source, target, send, recv, device):
        return pltpu.make_async_remote_copy(
            src_ref=source, dst_ref=target, send_sem=send, recv_sem=recv, device_id=device, device_id_type=MESH
        )

    def wait_for(buffer, semaphore):
        pltpu.make_async_copy(buffer, buffer, semaphore).wait()

    sibling = at(x, y, zq, zp, other)
    barrier = pltpu.get_barrier_semaphore()
    partners = [at(x, (y + ky) % 4, zq, zp, (c + kc) % 2) for ky, kc in ACROSS]
    partners += [near(kx, 0) for kx in (2, 1, 3)] + [near(0, 1), along(1), along(7)]
    partners += [at(x, y, (zq + k) % 8, 1 - zp, c) for k in (1, 7)]
    for partner in partners:
        signal(barrier, partner)

    own_half = pl.ds(pl.multiple_of(c * HALF, HALF), HALF)
    other_half = pl.ds(pl.multiple_of(other * HALF, HALF), HALF)
    own_head = pl.ds(pl.multiple_of(y * HD, HD), HD)
    load_keys = pltpu.make_async_copy(key_grad, keys, load_sem.at[0])
    load_normed = pltpu.make_async_copy(normed.at[:, own_half], tokens.at[c], load_sem.at[1])
    own_rows = pl.ds(pl.multiple_of(y * WIDE + c * HALF, HALF), HALF)
    load_weight = pltpu.make_async_copy(key_weight.at[own_rows], weights.at[:, own_head], load_sem.at[2])
    load_keys.start()
    load_normed.start()
    load_weight.start()
    load_keys.wait()
    first_row = (dx * 8 + dy) * ROWS
    raw[c, :, own_head] = rope_back(keys[...], first_row).astype(jnp.bfloat16)

    pl.semaphore_wait(barrier, len(partners))

    raw_copies = [
        remote(raw.at[c, :, own_head], raw.at[c, :, own_head], raw_send.at[i], raw_recv.at[i],
               at(x, (y + ky) % 4, zq, zp, (c + kc) % 2))
        for i, (ky, kc) in enumerate(ACROSS)
    ]
    for copy in raw_copies:
        copy.start()
    normed_copy = remote(normed.at[:, other_half], tokens.at[c], normed_send, normed_recv, sibling)
    normed_copy.start()
    for k in (1, 7):
        signal(one_away, along(k))
    load_normed.wait()
    normed_copy.wait_recv()
    turned[...] = tokens[...].reshape(2 * ROWS, HALF).T.reshape(8, GROUPS, 16, 2 * ROWS)
    pl.semaphore_wait(one_away, 2)
    for k in (2, 6):
        signal(two_away, along(k))
    raw_copies[-1].wait_recv()
    step = 1 + 2 * pair
    order = [(group + 2) % 4, (group + step) % 4, (group + 4 - step) % 4, group]
    raw_head = raw[:, :, own_head].astype(jnp.float32).reshape(2 * ROWS, HD)
    bias_near[x] = jnp.sum(raw_head, axis=0, keepdims=True)
    for copy in raw_copies[:-1]:
        copy.wait_recv()

    farther = [(pair, 1 - pair), (1 - pair, pair)]
    columns_of = [[pl.ds(pl.multiple_of(h * 2 * HD, 2 * HD), 2 * HD) for h in both] for both in farther]

    for j, g in enumerate(order):
        product = jnp.dot(
            turned[:, g].reshape(8 * 16, 2 * ROWS), raw[...].reshape(2 * ROWS, HEADS * HD),
            preferred_element_type=jnp.float32,
        )
        parts[:, g] = product.astype(jnp.bfloat16).reshape(8, 16, HEADS * HD)
        for h, columns in enumerate(columns_of[j] if j < 2 else [pl.ds(0, HEADS * HD)]):
            i = j * 2 + h if j < 2 else j + 2
            for kx in (2, 1, 3):
                remote(parts.at[pl.ds(((x + kx) % 4) * 2, 2), g, :, columns], got.at[x, :, g, :, columns],
                       near_send.at[i], near_recv.at[i], near(kx, 0)).start()
        if j == 0:
            for kx in (2, 1, 3):
                remote(bias_near.at[x], bias_near.at[x], bias_send.at[0], bias_recv.at[0], near(kx, 0)).start()
    got[x] = parts[pl.ds(x * 2, 2)]

    pl.semaphore_wait(two_away, 2)
    for j, g in enumerate(order):
        if j < 2:
            for i, (h, columns) in enumerate(zip(farther[j], columns_of[j])):
                wait_for(got.at[pl.ds(0, 3), :, g, :, columns], near_recv.at[j * 2 + i])
                total = got[0, :, g, :, columns].astype(jnp.float32)
                for s in range(1, 4):
                    total += got[s, :, g, :, columns].astype(jnp.float32)
                there = g * 2 + h
                halves[pl.ds(there * 2, 2)] = total.astype(jnp.bfloat16)
                for p in (1 - zp, zp):
                    remote(halves.at[there * 2 + p], got_far.at[z], far_send, far_recv, at(x, y, there, p, c)).start()
        else:
            wait_for(got.at[pl.ds(0, 3), :, g], near_recv.at[j + 2])
            total = got[0, :, g].astype(jnp.float32)
            for s in range(1, 4):
                total += got[s, :, g].astype(jnp.float32)
            total = total.astype(jnp.bfloat16)
            for h in range(2):
                halves[pl.ds((g * 2 + h) * 2, 2)] = total[:, :, h * 256:h * 256 + 256]
            for h, p in ((pair, 1 - zp), (pair, zp), (1 - pair, zp), (1 - pair, 1 - zp)):
                if j == 3 and h is pair and p is zp:
                    continue
                there = g * 2 + h
                remote(halves.at[there * 2 + p], got_far.at[z], far_send, far_recv, at(x, y, there, p, c)).start()
        if j == GROUPS - 1:
            wait_for(bias_near.at[pl.ds(0, 3)], bias_recv.at[0])
            bias_far[z] = bias_near[0] + bias_near[1] + bias_near[2] + bias_near[3]
            for k in (8, 7, 9, 6, 10, 5, 11, 4, 12, 3, 13, 2, 14, 1, 15):
                there = (z + k) % 16
                remote(bias_far.at[z], bias_far.at[z], bias_send.at[1], bias_recv.at[1],
                       at(x, y, there // 2, there % 2, c)).start()
    got_far[z] = halves[z]

    weight_copies = []
    for i, ky in enumerate((2, 1, 3)):
        there = (y + ky) % 4
        rows = pl.ds(pl.multiple_of(there * WIDE + c * HALF, HALF), HALF)
        weight_copies.append(
            remote(key_weight.at[rows], weights.at[:, own_head], weight_send.at[i], weight_recv.at[i],
                   at(x, there, zq, zp, c))
        )
    for copy in weight_copies:
        copy.start()

    wait_for(got_far.at[pl.ds(0, 15)], far_recv)
    final = got_far[0].astype(jnp.float32)
    for s in range(1, 16):
        final += got_far[s].astype(jnp.float32)
    final = (final * (1.0 / 128.0)).astype(jnp.bfloat16)
    tile[0] = final[:, :HD]
    tile[1] = final[:, HD:]

    target = weight_grad.at[y, c, xz, group]
    tile_copies = []
    for k in FAR + [0]:
        for h in range(2):
            there = pair * 2 + h
            copy = remote(tile.at[h], target, tile_send.at[len(tile_copies)], tile_recv.at[group],
                          at(x, there, (zq + k) % 8, zp, c))
            tile_copies.append((copy, k, there))
    own_tiles = [pltpu.make_async_copy(tile.at[h], target, tile_recv.at[group]) for h in range(2)]
    for copy, k, there in tile_copies:
        if k:
            copy.start()
        else:
            pl.when(there != y)(copy.start)
    for h in range(2):
        pl.when(pair * 2 + h == y)(own_tiles[h].start)

    wait_for(bias_far.at[pl.ds(0, 15)], bias_recv.at[1])
    bias_all = bias_far[0]
    for s in range(1, 16):
        bias_all += bias_far[s]
    bias_grad[...] = bias_all * (1.0 / 128.0)

    load_weight.wait()
    for copy in weight_copies:
        copy.wait_recv()
    result = lax.dot_general(
        raw[...].reshape(2 * ROWS, HEADS * HD), weights[...],
        (((1,), (1,)), ((), ())), preferred_element_type=jnp.float32,
    )
    inputs[...] = result.astype(jnp.bfloat16).reshape(2, ROWS, HALF)
    input_copy = remote(inputs.at[other], input_grad.at[:, own_half], input_send, input_recv, sibling)
    input_copy.start()
    input_local = pltpu.make_async_copy(inputs.at[c], input_grad.at[:, own_half], input_own)
    input_local.start()

    for copy in raw_copies + [normed_copy] + weight_copies:
        copy.wait_send()
    for i in range(4):
        wait_for(parts.at[pl.ds(0, 6), 0, :, pl.ds(0, 2 * HD)], near_send.at[i])
    for j in range(2, GROUPS):
        wait_for(parts.at[pl.ds(0, 6), 0], near_send.at[j + 2])
    wait_for(halves.at[pl.ds(0, 15)], far_send)
    wait_for(bias_near.at[pl.ds(0, 3)], bias_send.at[0])
    wait_for(bias_far.at[pl.ds(0, 15)], bias_send.at[1])

    arrivals = [group, (group + 4 - step) % 4, (group + step) % 4, (group + 2) % 4]
    last = GROUPS - 1
    for j, g in enumerate(arrivals):
        block = weight_grad.at[:, c, xz, g]
        wait_for(block, tile_recv.at[g])
        for kx, kz in NEAR:
            if j == last:
                there = at((x + kx) % 4, y, zq, (zp + kz) % 2, other)
                remote(block, block, cross_send, cross_recv, there).start()
            remote(block, block, wide_send.at[j], wide_recv.at[j], near(kx, kz)).start()
        if j == last:
            remote(block, block, cross_send, cross_recv, sibling).start()
    for copy, k, there in tile_copies:
        if k:
            copy.wait_send()
        else:
            pl.when(there != y)(copy.wait_send)
    for j, g in enumerate(arrivals[:last]):
        wait_for(weight_grad.at[:, c, pl.ds(0, 7), g], wide_recv.at[j])
        block = weight_grad.at[:, c, :, g]
        remote(block, block, core_send.at[j], core_recv.at[j], sibling).start()
    for j, g in enumerate(arrivals):
        wait_for(weight_grad.at[:, c, pl.ds(0, 7), g], wide_send.at[j])
    input_copy.wait()
    input_local.wait()
    for j, g in enumerate(arrivals[:last]):
        wait_for(weight_grad.at[:, c, :, g], core_send.at[j])
        wait_for(weight_grad.at[:, other, :, g], core_recv.at[j])
    far = arrivals[last]
    wait_for(weight_grad.at[:, c, :, far], cross_send)
    wait_for(weight_grad.at[:, c, pl.ds(0, 7), far], wide_recv.at[last])
    wait_for(weight_grad.at[:, other, :, far], cross_recv)


def finish(input_vmem, weight_vmem, bias_vmem, input_grad, weight_grad, bias_grad, done):
    copies = [
        pltpu.make_async_copy(weight_vmem, weight_grad, done.at[0]),
        pltpu.make_async_copy(input_vmem, input_grad, done.at[1]),
        pltpu.make_async_copy(bias_vmem, bias_grad, done.at[2]),
    ]
    for copy in copies:
        copy.start()
    for copy in copies:
        copy.wait()


def body(normed, key_weight, key_grad):
    dma, regular = pltpu.SemaphoreType.DMA, pltpu.SemaphoreType.REGULAR
    bf16, f32 = jnp.bfloat16, jnp.float32
    hbm = pl.BlockSpec(memory_space=pltpu.HBM)
    anywhere = pl.BlockSpec(memory_space=pl.ANY)
    local = pl.BlockSpec(memory_space=pltpu.VMEM)
    shapes = (
        jax.ShapeDtypeStruct((ROWS, WIDE), bf16),
        jax.ShapeDtypeStruct((4, 2, 8, GROUPS, 16, HD), bf16),
        jax.ShapeDtypeStruct((1, HD), f32),
    )
    normed, key_weight, key_grad = (pltpu.with_memory_space_constraint(a, pltpu.HBM) for a in (normed, key_weight, key_grad))
    results = pl.pallas_call(
        kernel,
        out_shape=shapes,
        in_specs=[hbm] * 3,
        out_specs=(anywhere, anywhere, local),
        scratch_shapes=[
            pltpu.VMEM((ROWS, HD), bf16),
            pltpu.VMEM((2, ROWS, HALF), bf16),
            pltpu.VMEM((8, GROUPS, 16, 2 * ROWS), bf16),
            pltpu.VMEM((2, ROWS, HEADS * HD), bf16),
            pltpu.VMEM((HALF, HEADS * HD), bf16),
            pltpu.VMEM((8, GROUPS, 16, HEADS * HD), bf16),
            pltpu.VMEM((4, 2, GROUPS, 16, HEADS * HD), bf16),
            pltpu.VMEM((16, 16, 2 * HD), bf16),
            pltpu.VMEM((16, 16, 2 * HD), bf16),
            pltpu.VMEM((2, 16, HD), bf16),
            pltpu.VMEM((2, ROWS, HALF), bf16),
            pltpu.VMEM((4, 1, HD), f32),
            pltpu.VMEM((16, 1, HD), f32),
            dma((3,)), dma((7,)), dma((7,)), dma, dma, dma((3,)), dma((3,)),
            dma((6,)), dma((6,)), dma, dma, dma((16,)), dma((4,)), dma((4,)), dma((4,)),
            dma((3,)), dma((3,)), dma, dma, dma,
            dma, dma, dma((2,)), dma((2,)), regular, regular,
        ],
        compiler_params=pltpu.CompilerParams(collective_id=0, has_side_effects=True, vmem_limit_bytes=32 << 20),
        cost_estimate=pl.CostEstimate(flops=4 * 256 * 512 * 512, bytes_accessed=4 << 20, transcendentals=0),
        name="key_projection_backward",
    )(normed, key_weight, key_grad)
    input_grad, weight_grad, bias_grad = pl.pallas_call(
        finish,
        out_shape=shapes,
        in_specs=[anywhere] * 3,
        out_specs=(hbm,) * 3,
        scratch_shapes=[dma((3,))],
        compiler_params=pltpu.CompilerParams(vmem_limit_bytes=1 << 20),
        name="write_results",
    )(*results)
    return input_grad, weight_grad.reshape(4096, HD), bias_grad.reshape(HD)


def solution(mesh):
    placed = (P(("dx", "dy"), "tp"), P(None, "tp"), P(("dx", "dy"), "tp"))
    return jax.shard_map(
        body,
        mesh=mesh,
        in_specs=placed,
        out_specs=(P(("dx", "dy"), "tp"), P(None, "tp"), P("tp")),
        check_vma=False,
    )
```

```python
import math

import jax
import jax.numpy as jnp
from jax import lax
from jax.experimental import pallas as pl
from jax.experimental.pallas import tpu as pltpu
from jax.sharding import PartitionSpec as P

HD = 128
SEQ = 4096
HEADS = 4
ROWS = 128
WIDE = 1024
HALF = 512
MESH = pl.DeviceIdType.MESH
NEAR = [(kx, kz) for kz in range(2) for kx in range(4) if (kx, kz) != (0, 0)]
NEAR.sort(key=lambda k: -(min(k[0], 4 - k[0]) + k[1]))
ACROSS = [(ky, kc) for ky in (2, 1, 3, 0) for kc in (1, 0) if (ky, kc) != (0, 0)]
FAR = [4, 3, 5, 2, 6, 1, 7]
GROUPS = 4


def rope_back(grad, first_row):
    values = grad.astype(jnp.float32)
    row = lax.broadcasted_iota(jnp.int32, (ROWS, HD), 0)
    lane = lax.broadcasted_iota(jnp.int32, (ROWS, HD), 1)
    positions = ((first_row + row) % SEQ).astype(jnp.float32)
    place = jnp.where(lane < HD // 2, lane, lane - HD // 2).astype(jnp.float32)
    angles = positions * jnp.exp(place * (-2.0 * math.log(1000000.0) / HD))
    sines = jnp.sin(angles)
    sines = jnp.where(lane < HD // 2, sines, -sines)
    return values * jnp.cos(angles) + pltpu.roll(values, HD // 2, 1) * sines


def kernel(
    normed, key_weight, key_grad, input_grad, weight_grad, bias_grad,
    keys, tokens, turned, raw, weights, parts, got, halves, got_far, tile, inputs, bias_near, bias_far,
    load_sem, raw_send, raw_recv, normed_send, normed_recv, weight_send, weight_recv,
    near_send, near_recv, far_send, far_recv, tile_send, tile_recv, wide_send, wide_recv,
    core_send, core_recv, input_send, input_recv, input_own,
    cross_send, cross_recv, bias_send, bias_recv, one_away, two_away,
):
    dx, dy, y = lax.axis_index("dx"), lax.axis_index("dy"), lax.axis_index("tp")
    x, c = dy % 4, dx % 2
    z = (dy // 4) * 8 + dx // 2
    zp, zq = z % 2, z // 2
    xz = x * 2 + zp
    group, pair = zq // 2, zq % 2
    other = 1 - c

    def at(x, y, zq, zp, c):
        z = zq * 2 + zp
        return ((z % 8) * 2 + c, (z // 8) * 4 + x, y)

    def along(k):
        return at(x, y, (zq + k) % 8, zp, c)

    def near(kx, kz):
        return at((x + kx) % 4, y, zq, (zp + kz) % 2, c)

    def signal(semaphore, device):
        pl.semaphore_signal(semaphore, inc=1, device_id=device, device_id_type=MESH)

    def remote(source, target, send, recv, device):
        return pltpu.make_async_remote_copy(
            src_ref=source, dst_ref=target, send_sem=send, recv_sem=recv, device_id=device, device_id_type=MESH
        )

    def wait_for(buffer, semaphore):
        pltpu.make_async_copy(buffer, buffer, semaphore).wait()

    sibling = at(x, y, zq, zp, other)
    barrier = pltpu.get_barrier_semaphore()
    partners = [at(x, (y + ky) % 4, zq, zp, (c + kc) % 2) for ky, kc in ACROSS]
    partners += [near(kx, 0) for kx in (2, 1, 3)] + [near(0, 1), along(1), along(7)]
    partners += [at(x, y, (zq + k) % 8, 1 - zp, c) for k in (1, 7)]
    for partner in partners:
        signal(barrier, partner)

    own_half = pl.ds(pl.multiple_of(c * HALF, HALF), HALF)
    other_half = pl.ds(pl.multiple_of(other * HALF, HALF), HALF)
    own_head = pl.ds(pl.multiple_of(y * HD, HD), HD)
    load_keys = pltpu.make_async_copy(key_grad, keys, load_sem.at[0])
    load_normed = pltpu.make_async_copy(normed.at[:, own_half], tokens.at[c], load_sem.at[1])
    own_rows = pl.ds(pl.multiple_of(y * WIDE + c * HALF, HALF), HALF)
    load_weight = pltpu.make_async_copy(key_weight.at[own_rows], weights.at[:, own_head], load_sem.at[2])
    load_keys.start()
    load_normed.start()
    load_weight.start()
    load_keys.wait()
    first_row = (dx * 8 + dy) * ROWS
    raw[c, :, own_head] = rope_back(keys[...], first_row).astype(jnp.bfloat16)

    pl.semaphore_wait(barrier, len(partners))

    raw_copies = [
        remote(raw.at[c, :, own_head], raw.at[c, :, own_head], raw_send.at[i], raw_recv.at[i],
               at(x, (y + ky) % 4, zq, zp, (c + kc) % 2))
        for i, (ky, kc) in enumerate(ACROSS)
    ]
    for copy in raw_copies:
        copy.start()
    normed_copy = remote(normed.at[:, other_half], tokens.at[c], normed_send, normed_recv, sibling)
    normed_copy.start()
    for k in (1, 7):
        signal(one_away, along(k))
    load_normed.wait()
    normed_copy.wait_recv()
    turned[...] = tokens[...].reshape(2 * ROWS, HALF).T.reshape(8, GROUPS, 16, 2 * ROWS)
    pl.semaphore_wait(one_away, 2)
    for k in (2, 6):
        signal(two_away, along(k))
    raw_copies[-1].wait_recv()
    step = 1 + 2 * pair
    order = [(group + 2) % 4, (group + step) % 4, (group + 4 - step) % 4, group]
    raw_head = raw[:, :, own_head].astype(jnp.float32).reshape(2 * ROWS, HD)
    bias_near[x] = jnp.sum(raw_head, axis=0, keepdims=True)
    for copy in raw_copies[:-1]:
        copy.wait_recv()

    farther = [(pair, 1 - pair), (1 - pair, pair)]
    columns_of = [[pl.ds(pl.multiple_of(h * 2 * HD, 2 * HD), 2 * HD) for h in both] for both in farther]

    for j, g in enumerate(order):
        product = jnp.dot(
            turned[:, g].reshape(8 * 16, 2 * ROWS), raw[...].reshape(2 * ROWS, HEADS * HD),
            preferred_element_type=jnp.float32,
        )
        parts[:, g] = product.astype(jnp.bfloat16).reshape(8, 16, HEADS * HD)
        for h, columns in enumerate(columns_of[j] if j < 2 else [pl.ds(0, HEADS * HD)]):
            i = j * 2 + h if j < 2 else j + 2
            for kx in (2, 1, 3):
                remote(parts.at[pl.ds(((x + kx) % 4) * 2, 2), g, :, columns], got.at[x, :, g, :, columns],
                       near_send.at[i], near_recv.at[i], near(kx, 0)).start()
        if j == 0:
            for kx in (2, 1, 3):
                remote(bias_near.at[x], bias_near.at[x], bias_send.at[0], bias_recv.at[0], near(kx, 0)).start()
    got[x] = parts[pl.ds(x * 2, 2)]

    pl.semaphore_wait(two_away, 2)
    for j, g in enumerate(order):
        if j < 2:
            for i, (h, columns) in enumerate(zip(farther[j], columns_of[j])):
                wait_for(got.at[pl.ds(0, 3), :, g, :, columns], near_recv.at[j * 2 + i])
                total = got[0, :, g, :, columns].astype(jnp.float32)
                for s in range(1, 4):
                    total += got[s, :, g, :, columns].astype(jnp.float32)
                there = g * 2 + h
                halves[pl.ds(there * 2, 2)] = total.astype(jnp.bfloat16)
                for p in (1 - zp, zp):
                    remote(halves.at[there * 2 + p], got_far.at[z], far_send, far_recv, at(x, y, there, p, c)).start()
        else:
            wait_for(got.at[pl.ds(0, 3), :, g], near_recv.at[j + 2])
            total = got[0, :, g].astype(jnp.float32)
            for s in range(1, 4):
                total += got[s, :, g].astype(jnp.float32)
            total = total.astype(jnp.bfloat16)
            for h in range(2):
                halves[pl.ds((g * 2 + h) * 2, 2)] = total[:, :, h * 256:h * 256 + 256]
            for h, p in ((pair, 1 - zp), (pair, zp), (1 - pair, zp), (1 - pair, 1 - zp)):
                if j == 3 and h is pair and p is zp:
                    continue
                there = g * 2 + h
                remote(halves.at[there * 2 + p], got_far.at[z], far_send, far_recv, at(x, y, there, p, c)).start()
        if j == GROUPS - 1:
            wait_for(bias_near.at[pl.ds(0, 3)], bias_recv.at[0])
            bias_far[z] = bias_near[0] + bias_near[1] + bias_near[2] + bias_near[3]
            for k in (8, 7, 9, 6, 10, 5, 11, 4, 12, 3, 13, 2, 14, 1, 15):
                there = (z + k) % 16
                remote(bias_far.at[z], bias_far.at[z], bias_send.at[1], bias_recv.at[1],
                       at(x, y, there // 2, there % 2, c)).start()
    got_far[z] = halves[z]

    weight_copies = []
    for i, ky in enumerate((2, 1, 3)):
        there = (y + ky) % 4
        rows = pl.ds(pl.multiple_of(there * WIDE + c * HALF, HALF), HALF)
        weight_copies.append(
            remote(key_weight.at[rows], weights.at[:, own_head], weight_send.at[i], weight_recv.at[i],
                   at(x, there, zq, zp, c))
        )
    for copy in weight_copies:
        copy.start()

    wait_for(got_far.at[pl.ds(0, 15)], far_recv)
    final = got_far[0].astype(jnp.float32)
    for s in range(1, 16):
        final += got_far[s].astype(jnp.float32)
    final = (final * (1.0 / 128.0)).astype(jnp.bfloat16)
    tile[0] = final[:, :HD]
    tile[1] = final[:, HD:]

    target = weight_grad.at[y, c, xz, group]
    tile_copies = []
    for k in FAR + [0]:
        for h in range(2):
            there = pair * 2 + h
            copy = remote(tile.at[h], target, tile_send.at[len(tile_copies)], tile_recv.at[group],
                          at(x, there, (zq + k) % 8, zp, c))
            tile_copies.append((copy, k, there))
    own_tiles = [pltpu.make_async_copy(tile.at[h], target, tile_recv.at[group]) for h in range(2)]
    for copy, k, there in tile_copies:
        if k:
            copy.start()
        else:
            pl.when(there != y)(copy.start)
    for h in range(2):
        pl.when(pair * 2 + h == y)(own_tiles[h].start)

    load_weight.wait()
    for copy in weight_copies:
        copy.wait_recv()
    result = lax.dot_general(
        raw[...].reshape(2 * ROWS, HEADS * HD), weights[...],
        (((1,), (1,)), ((), ())), preferred_element_type=jnp.float32,
    )
    inputs[...] = result.astype(jnp.bfloat16).reshape(2, ROWS, HALF)
    input_copy = remote(inputs.at[other], input_grad.at[:, own_half], input_send, input_recv, sibling)
    input_copy.start()
    input_local = pltpu.make_async_copy(inputs.at[c], input_grad.at[:, own_half], input_own)
    input_local.start()

    for copy in raw_copies + [normed_copy] + weight_copies:
        copy.wait_send()
    for i in range(4):
        wait_for(parts.at[pl.ds(0, 6), 0, :, pl.ds(0, 2 * HD)], near_send.at[i])
    for j in range(2, GROUPS):
        wait_for(parts.at[pl.ds(0, 6), 0], near_send.at[j + 2])
    wait_for(halves.at[pl.ds(0, 15)], far_send)
    wait_for(bias_near.at[pl.ds(0, 3)], bias_send.at[0])
    wait_for(bias_far.at[pl.ds(0, 15)], bias_send.at[1])

    arrivals = [group, (group + 4 - step) % 4, (group + step) % 4, (group + 2) % 4]
    last = GROUPS - 1
    for j, g in enumerate(arrivals):
        block = weight_grad.at[:, c, xz, g]
        wait_for(block, tile_recv.at[g])
        for kx, kz in NEAR:
            if j == last:
                there = at((x + kx) % 4, y, zq, (zp + kz) % 2, other)
                remote(block, block, cross_send, cross_recv, there).start()
            remote(block, block, wide_send.at[j], wide_recv.at[j], near(kx, kz)).start()
        if j == last:
            remote(block, block, cross_send, cross_recv, sibling).start()
    wait_for(bias_far.at[pl.ds(0, 15)], bias_recv.at[1])
    bias_all = bias_far[0]
    for s in range(1, 16):
        bias_all += bias_far[s]
    bias_grad[...] = bias_all * (1.0 / 128.0)
    for copy, k, there in tile_copies:
        if k:
            copy.wait_send()
        else:
            pl.when(there != y)(copy.wait_send)
    for j, g in enumerate(arrivals[:last]):
        wait_for(weight_grad.at[:, c, pl.ds(0, 7), g], wide_recv.at[j])
        block = weight_grad.at[:, c, :, g]
        remote(block, block, core_send.at[j], core_recv.at[j], sibling).start()
    for j, g in enumerate(arrivals):
        wait_for(weight_grad.at[:, c, pl.ds(0, 7), g], wide_send.at[j])
    input_copy.wait()
    input_local.wait()
    for j, g in enumerate(arrivals[:last]):
        wait_for(weight_grad.at[:, c, :, g], core_send.at[j])
        wait_for(weight_grad.at[:, other, :, g], core_recv.at[j])
    far = arrivals[last]
    wait_for(weight_grad.at[:, c, :, far], cross_send)
    wait_for(weight_grad.at[:, c, pl.ds(0, 7), far], wide_recv.at[last])
    wait_for(weight_grad.at[:, other, :, far], cross_recv)


def finish(input_vmem, weight_vmem, bias_vmem, input_grad, weight_grad, bias_grad, done):
    copies = [
        pltpu.make_async_copy(weight_vmem, weight_grad, done.at[0]),
        pltpu.make_async_copy(input_vmem, input_grad, done.at[1]),
        pltpu.make_async_copy(bias_vmem, bias_grad, done.at[2]),
    ]
    for copy in copies:
        copy.start()
    for copy in copies:
        copy.wait()


def body(normed, key_weight, key_grad):
    dma, regular = pltpu.SemaphoreType.DMA, pltpu.SemaphoreType.REGULAR
    bf16, f32 = jnp.bfloat16, jnp.float32
    hbm = pl.BlockSpec(memory_space=pltpu.HBM)
    anywhere = pl.BlockSpec(memory_space=pl.ANY)
    local = pl.BlockSpec(memory_space=pltpu.VMEM)
    shapes = (
        jax.ShapeDtypeStruct((ROWS, WIDE), bf16),
        jax.ShapeDtypeStruct((4, 2, 8, GROUPS, 16, HD), bf16),
        jax.ShapeDtypeStruct((1, HD), f32),
    )
    normed, key_weight, key_grad = (pltpu.with_memory_space_constraint(a, pltpu.HBM) for a in (normed, key_weight, key_grad))
    results = pl.pallas_call(
        kernel,
        out_shape=shapes,
        in_specs=[hbm] * 3,
        out_specs=(anywhere, anywhere, local),
        scratch_shapes=[
            pltpu.VMEM((ROWS, HD), bf16),
            pltpu.VMEM((2, ROWS, HALF), bf16),
            pltpu.VMEM((8, GROUPS, 16, 2 * ROWS), bf16),
            pltpu.VMEM((2, ROWS, HEADS * HD), bf16),
            pltpu.VMEM((HALF, HEADS * HD), bf16),
            pltpu.VMEM((8, GROUPS, 16, HEADS * HD), bf16),
            pltpu.VMEM((4, 2, GROUPS, 16, HEADS * HD), bf16),
            pltpu.VMEM((16, 16, 2 * HD), bf16),
            pltpu.VMEM((16, 16, 2 * HD), bf16),
            pltpu.VMEM((2, 16, HD), bf16),
            pltpu.VMEM((2, ROWS, HALF), bf16),
            pltpu.VMEM((4, 1, HD), f32),
            pltpu.VMEM((16, 1, HD), f32),
            dma((3,)), dma((7,)), dma((7,)), dma, dma, dma((3,)), dma((3,)),
            dma((6,)), dma((6,)), dma, dma, dma((16,)), dma((4,)), dma((4,)), dma((4,)),
            dma((3,)), dma((3,)), dma, dma, dma,
            dma, dma, dma((2,)), dma((2,)), regular, regular,
        ],
        compiler_params=pltpu.CompilerParams(collective_id=0, has_side_effects=True, vmem_limit_bytes=32 << 20),
        cost_estimate=pl.CostEstimate(flops=4 * 256 * 512 * 512, bytes_accessed=4 << 20, transcendentals=0),
        name="key_projection_backward",
    )(normed, key_weight, key_grad)
    input_grad, weight_grad, bias_grad = pl.pallas_call(
        finish,
        out_shape=shapes,
        in_specs=[anywhere] * 3,
        out_specs=(hbm,) * 3,
        scratch_shapes=[dma((3,))],
        compiler_params=pltpu.CompilerParams(vmem_limit_bytes=1 << 20),
        name="write_results",
    )(*results)
    return input_grad, weight_grad.reshape(4096, HD), bias_grad.reshape(HD)


def solution(mesh):
    placed = (P(("dx", "dy"), "tp"), P(None, "tp"), P(("dx", "dy"), "tp"))
    return jax.shard_map(
        body,
        mesh=mesh,
        in_specs=placed,
        out_specs=(P(("dx", "dy"), "tp"), P(None, "tp"), P("tp")),
        check_vma=False,
    )
```
